128 devices in a mesh: gx: 32 (over z, y, core), gy: 2 (over x_hi), gz: 2 (over x_lo).
Axes of the slice: x: 4 (x_hi: 2, x_lo: 2; x = x_hi * 2 + x_lo), y: 4, z: 4, core: 2. Of those that a mesh axis runs over, the one named last changes fastest.
Arguments:
- position: float32 [3, 512, 8, 8, 256], P(None, 'gx', 'gy', 'gz'), may hold values from 0 to 1
- velocity: float32 [3, 512, 8, 8, 256], P(None, 'gx', 'gy', 'gz'), may hold values from -6 to 6
- particle_mass: float32 [512, 8, 8, 256], P('gx', 'gy', 'gz'), may hold values from 0.001953125 to 0.0078125
- smoothing: float32 [512, 8, 8, 256], P('gx', 'gy', 'gz'), may hold values from 0.2 to 0.5
- entropy: float32 [512, 8, 8, 256], P('gx', 'gy', 'gz'), may hold values from 0.5 to 2
- stored_density: float32 [512, 8, 8, 256], P('gx', 'gy', 'gz'), may hold values from 0.3 to 2
- particle_count: int32 [512, 8, 8], P('gx', 'gy', 'gz'), may hold values from 64 to 256, as said below
- active_count: int32 [512, 8, 8], P('gx', 'gy', 'gz'), may hold values from 0 to 8, as said below
- pair_side: int32 [26, 512, 8, 8], P(None, 'gx', 'gy', 'gz'), may hold values from 0 to 2, as said below
Outputs:
- density: float32 [512, 8, 8, 256], P('gx', 'gy', 'gz')
- acceleration: float32 [3, 512, 8, 8, 256], P(None, 'gx', 'gy', 'gz')
The draws below stay inside these ranges and needn't reach their ends.
Inputs may be any that keep to these rules, and one draw needn't show every extreme that they name: `particle_count`: present particles fill the first slots of a cell. `active_count`: active particles fill the first slots of a cell; some cell has 8 of them. `pair_side`: 0: the pair does not interact; 1: this cell's side evaluates it; 2: the neighbour's side does. Entry k of cell a and entry 25 - k of the cell a + offset k agree: 0 with 0, 1 with 2, 2 with 1.
All inputs are finite; a program needn't handle non-finite values.
Results may differ from the reference program's by a relative error of at most 0.0003.
Values sent between devices are 32-bit elements; how exact they have to be, the bound alone decides.
No kernel may reach another device: no remote copies, remote signals or barrier semaphores. Data moves between devices by JAX's collectives and lax.ppermute only.
A program may use at most 320 MiB of HBM per device.

```python
import math
import jax
import jax.numpy as jnp
from jax import lax

SLOTS = 256
ACT = 8
NX = 512
NY = 8
NZ = 8


def neighbour_offsets_drawn():
    return [(a, b, c) for a in (-1, 0, 1) for b in (-1, 0, 1) for c in (-1, 0, 1) if (a, b, c) != (0, 0, 0)]


def draw_particle_count(key, part):
    key = jax.random.fold_in(key, 11)
    counted = jax.random.randint(key, (NX, NY, NZ), SLOTS // 4, SLOTS + 1)
    return counted.at[0, 0, 0].set(SLOTS).astype(jnp.int32)


def draw_active_count(key, part):
    key = jax.random.fold_in(key, 12)
    counted = jax.random.randint(key, (NX, NY, NZ), 0, ACT + 1)
    return counted.at[0, 0, 0].set(ACT).astype(jnp.int32)


def draw_pair_side(key, part):
    key = jax.random.fold_in(key, 13)
    offsets = neighbour_offsets_drawn()
    drawn_flags = jax.random.randint(key, (13, NX, NY, NZ), 0, 8)
    forward_flags = jnp.where(drawn_flags < 2, 0, jnp.where(drawn_flags < 5, 1, 2)).astype(jnp.int32)
    mirrored = jnp.where(forward_flags == 0, 0, 3 - forward_flags).astype(jnp.int32)
    flag_rows = [forward_flags[k] for k in range(13)] + [None] * 13
    for k in range(13):
        offset_cells = offsets[k]
        flag_rows[25 - k] = jnp.roll(mirrored[k], offset_cells, axis=(0, 1, 2))
    return jnp.stack(flag_rows, 0).astype(jnp.int32)


def steps_of(stream_key, extent, shards, low, largest):
    level, own = 1.0, jax.random.fold_in(stream_key, 6)
    for dim, blocks in shards:
        heights = jnp.exp(jax.random.uniform(jax.random.fold_in(own, dim), (blocks,), jnp.float32, low / len(shards), largest / len(shards)))
        level = level * jnp.repeat(heights, extent[dim] // blocks).reshape([-1 if axis == dim else 1 for axis in range(len(extent))])
    return level


def centred(key, extent, scale, limit, split=(), kind=jnp.bfloat16):
    drawn = jax.random.normal(key, extent, jnp.float32) * scale
    if len(split) > 0:
        drawn = steps_of(key, extent, split, -0.22, 0.18) * drawn
    return jnp.clip(drawn, min=-limit, max=limit).astype(kind)


def setup_inputs(seed: int = 0) -> dict:
    keys = jax.random.split(jax.random.key(seed), 10)
    position = jnp.clip(1.0 * jax.random.uniform(keys[0], (3, NX, NY, NZ, SLOTS), jnp.float32) ** steps_of(keys[0], (3, NX, NY, NZ, SLOTS), ((1, 32), (2, 2), (3, 2)), -0.2, 0.2), 0.0, 1.0)
    velocity = centred(keys[1], (3, NX, NY, NZ, SLOTS), 1.0, 6.0, ((1, 32), (2, 2), (3, 2)), jnp.float32)
    particle_mass = jnp.clip(jnp.exp(math.log(0.0078125) - 1.3862944 * jax.random.uniform(keys[2], (NX, NY, NZ, SLOTS), jnp.float32) ** steps_of(keys[2], (NX, NY, NZ, SLOTS), ((0, 32), (1, 2), (2, 2)), -0.2, 0.2)), 0.001953125, 0.0078125)
    smoothing = jnp.clip(jnp.exp(math.log(0.5) - 0.9162907 * jax.random.uniform(keys[3], (NX, NY, NZ, SLOTS), jnp.float32) ** steps_of(keys[3], (NX, NY, NZ, SLOTS), ((0, 32), (1, 2), (2, 2)), -0.2, 0.2)), 0.2, 0.5)
    entropy = jnp.clip(jnp.exp(math.log(2.0) - 1.3862944 * jax.random.uniform(keys[4], (NX, NY, NZ, SLOTS), jnp.float32) ** steps_of(keys[4], (NX, NY, NZ, SLOTS), ((0, 32), (1, 2), (2, 2)), -0.2, 0.2)), 0.5, 2.0)
    stored_density = jnp.clip(jnp.exp(math.log(2.0) - 1.89712 * jax.random.uniform(keys[5], (NX, NY, NZ, SLOTS), jnp.float32) ** steps_of(keys[5], (NX, NY, NZ, SLOTS), ((0, 32), (1, 2), (2, 2)), -0.2, 0.2)), 0.3, 2.0)
    particle_count = draw_particle_count(jax.random.fold_in(keys[9], 71), 0)
    active_count = draw_active_count(jax.random.fold_in(keys[9], 71), 0)
    pair_side = draw_pair_side(jax.random.fold_in(keys[9], 71), 0)
    return {"position": position, "velocity": velocity, "particle_mass": particle_mass, "smoothing": smoothing, "entropy": entropy, "stored_density": stored_density, "particle_count": particle_count, "active_count": active_count, "pair_side": pair_side}


ADIABATIC = 5.0 / 3.0
VISC_ALPHA = 1.0
VISC_BETA = 2.0

def neighbour_offsets():
    return [(a, b, c) for a in (-1, 0, 1) for b in (-1, 0, 1) for c in (-1, 0, 1) if (a, b, c) != (0, 0, 0)]

def kernel_value(distance_sq, smooth):
    scaled_dist = jnp.sqrt(distance_sq) / smooth
    profile = 0.25 * jnp.maximum(2.0 - scaled_dist, 0.0) ** 3 - jnp.maximum(1.0 - scaled_dist, 0.0) ** 3
    return profile / (math.pi * smooth ** 3)

def kernel_slope(distance_sq, smooth):
    scaled_dist = jnp.sqrt(distance_sq) / smooth
    profile = -0.75 * jnp.maximum(2.0 - scaled_dist, 0.0) ** 2 / jnp.maximum(scaled_dist, 1.0) - 0.75 * scaled_dist * jnp.maximum(1.0 - scaled_dist, 0.0)
    return profile / (math.pi * smooth ** 5)

def separation(row_fields, col_fields, toward):
    return [row_fields[c][..., :, None] - col_fields[c][..., None, :] - toward[c] for c in range(3)]

def density_tile(row_fields, col_fields, toward):
    components = separation(row_fields, col_fields, toward)
    distance_sq = components[0] ** 2 + components[1] ** 2 + components[2] ** 2
    weighted = col_fields[3][..., None, :] * kernel_value(distance_sq, row_fields[4][..., :, None])
    return lax.optimization_barrier(jnp.sum(weighted, axis=-1))[None]

def force_tile(row_fields, col_fields, toward):
    components = separation(row_fields, col_fields, toward)
    distance_sq = components[0] ** 2 + components[1] ** 2 + components[2] ** 2
    closing = sum(((row_fields[5 + c][..., :, None] - col_fields[5 + c][..., None, :]) * components[c] for c in range(3)))
    h_row = row_fields[4][..., :, None]
    h_col = col_fields[4][..., None, :]
    h_mean = 0.5 * (h_row + h_col)
    approach = h_mean * jnp.minimum(closing, 0.0) / (distance_sq + 0.01 * h_mean ** 2)
    sound_mean = 0.5 * (row_fields[10][..., :, None] + col_fields[10][..., None, :])
    rho_mean = 0.5 * (row_fields[8][..., :, None] + col_fields[8][..., None, :])
    viscosity = (-VISC_ALPHA * sound_mean * approach + VISC_BETA * approach ** 2) / rho_mean
    slope_row = kernel_slope(distance_sq, h_row)
    slope_col = kernel_slope(distance_sq, h_col)
    weighting = col_fields[3][..., None, :] * (row_fields[9][..., :, None] * slope_row + col_fields[9][..., None, :] * slope_col + 0.5 * viscosity * (slope_row + slope_col))
    return jnp.stack([-lax.optimization_barrier(jnp.sum(weighting * components[c], axis=-1)) for c in range(3)], 0)

def pair_sum(fields, pair_side, tile):
    padded = jnp.pad(fields, ((0, 0), (1, 1), (1, 1), (1, 1), (0, 0)), mode='wrap')
    offsets = neighbour_offsets()

    def one_slab(slab_index):
        home_fields = lax.dynamic_slice_in_dim(fields, slab_index, 1, 1)[:, 0]
        flags = lax.dynamic_slice_in_dim(pair_side, slab_index, 1, 1)[:, 0]
        row_fields = home_fields[..., :ACT]
        summed = tile(row_fields, home_fields, (0.0, 0.0, 0.0))
        for k, offset_cells in enumerate(offsets):
            slab = lax.dynamic_slice_in_dim(padded, slab_index + 1 + offset_cells[0], 1, 1)[:, 0]
            col_fields = slab[:, 1 + offset_cells[1]:1 + offset_cells[1] + NY, 1 + offset_cells[2]:1 + offset_cells[2] + NZ]
            contribution = tile(row_fields, col_fields, offset_cells)
            summed = summed + jnp.where(flags[k][..., None] != 0, contribution, 0.0)
        return summed
    mapped = lax.map(one_slab, jnp.arange(NX, dtype=jnp.int32))
    return jnp.moveaxis(mapped, 0, 1)

def reference(position, velocity, particle_mass, smoothing, entropy, stored_density, particle_count, active_count, pair_side):
    slot_index = lax.broadcasted_iota(jnp.int32, particle_mass.shape, 3)
    present = slot_index < particle_count[..., None]
    active = slot_index < active_count[..., None]
    mass_live = jnp.where(present, particle_mass, 0.0)
    fields = jnp.concatenate([position, mass_live[None], smoothing[None], velocity, entropy[None], stored_density[None]], 0)
    fresh_rho = pair_sum(fields, pair_side, density_tile)[0]
    widened = jnp.concatenate([fresh_rho, stored_density[..., ACT:]], -1)
    density = jnp.where(active, widened, stored_density)
    pressure = entropy * density ** (-1.0 / 3.0)
    sound_speed = jnp.sqrt(ADIABATIC * pressure * density)
    force_fields = jnp.concatenate([fields[:8], density[None], pressure[None], sound_speed[None]], 0)
    pushed = pair_sum(force_fields, pair_side, force_tile)
    padding = jnp.zeros(pushed.shape[:-1] + (SLOTS - ACT,), pushed.dtype)
    widened_push = jnp.concatenate([pushed, padding], -1)
    acceleration = jnp.where(active[None], widened_push, 0.0)
    return (density, acceleration)
```

```python
import functools
import math

import jax
import jax.numpy as jnp
import numpy as np
from jax import lax
from jax.experimental import pallas as pl
from jax.experimental.pallas import tpu as pltpu
from jax.sharding import PartitionSpec as P

ACT = 8
BX, BY, BZ = 16, 4, 4
CELLS = BX * BY * BZ
EX, EY, EZ = BX + 2, BY + 2, BZ + 2
EXT = EX * EY * EZ
LANES = 768
TILES = LANES // 128
GROUPS = 2 * LANES
ROWS = 112
FLAGS = 80
LIVE = 106
SPAN = 4
BATCH_D = 4
BATCH_F = 2
NONE = CELLS
ADIABATIC = 5.0 / 3.0
HIGHEST = lax.Precision.HIGHEST
f32 = jnp.float32
i32 = jnp.int32

OFFSETS = [
    (a, b, c) for a in (-1, 0, 1) for b in (-1, 0, 1) for c in (-1, 0, 1) if (a, b, c) != (0, 0, 0)
]


def maps():
    coord = np.full((8, LANES), -9, np.int32)
    coord[:3] = -5
    source = np.full((8, LANES), -1, np.int32)
    for x in range(-1, BX + 1):
        for y in range(-1, BY + 1):
            for z in range(-1, BZ + 1):
                lane = ((x + 1) * EY + y + 1) * EZ + z + 1
                coord[0, lane], coord[1, lane], coord[2, lane] = x, y, z
                inside_y, inside_z = 0 <= y < BY, 0 <= z < BZ
                face_y = 0 if y == BY else 1
                face_z = 0 if z == BZ else 1
                def place(width_home, width_y, width_z, width_yz, starts, row):
                    if inside_y and inside_z:
                        return starts[0] + row * width_home + y * BZ + z
                    if inside_z:
                        return starts[1] + row * width_y + face_y * BZ + z
                    if inside_y:
                        return starts[2] + row * width_z + y * 2 + face_z
                    return starts[3] + row * width_yz + face_y * 2 + face_z

                if 0 <= x < BX:
                    at = place(16, 8, 8, 4, (0, 256, 384, 512), x)
                else:
                    base = 576 if x < 0 else 612
                    at = place(16, 8, 8, 4, (base, base + 16, base + 24, base + 32), 0)
                source[0, lane] = at
    return coord, source


def sent_cells():
    table = np.full((8, 384), -1, np.int32)
    for x in range(BX):
        for face in range(2):
            for z in range(BZ):
                table[0, x * 8 + face * BZ + z] = (x * BY + (0 if face == 0 else BY - 1)) * BZ + z
            for y in range(BY):
                table[0, 128 + x * 8 + y * 2 + face] = (x * BY + y) * BZ + (
                    0 if face == 0 else BZ - 1
                )
            for other in range(2):
                table[0, 256 + x * 4 + face * 2 + other] = (
                    x * BY + (0 if face == 0 else BY - 1)
                ) * BZ + (0 if other == 0 else BZ - 1)
    return table


def picked(values, source_row):
    size = values.shape[1]
    rows = lax.broadcasted_iota(i32, (size, source_row.shape[1]), 0)
    chosen = (rows == source_row).astype(f32)
    return lax.dot_general(
        values, chosen, (((1,), (0,)), ((), ())), precision=HIGHEST, preferred_element_type=f32
    )


def unit_rows():
    return (
        lax.broadcasted_iota(i32, (ACT, 128), 0) == lax.broadcasted_iota(i32, (ACT, 128), 1)
    ).astype(f32)


def cells_to_lanes(natural):
    return lax.dot_general(
        unit_rows(), natural[:, :128], (((1,), (1,)), ((), ())), precision=HIGHEST,
        preferred_element_type=f32,
    )


def lanes_to_cells(rows):
    return lax.dot_general(
        rows, unit_rows(), (((0,), (0,)), ((), ())), precision=HIGHEST, preferred_element_type=f32
    )


def live_mass(mass, count):
    slot = lax.broadcasted_iota(i32, (CELLS, 256), 1)
    return jnp.where(slot < count, mass, 0.0)


def pack_kernel(pos, vel, mass, smooth, entropy, stored, count, flags, sent, table, faces):
    fields = [pos[c].reshape(CELLS, 256) for c in range(3)]
    fields.append(live_mass(mass[...].reshape(CELLS, 256), count[...]))
    fields.append(smooth[...].reshape(CELLS, 256))
    fields += [vel[c].reshape(CELLS, 256) for c in range(3)]
    fields += [entropy[...].reshape(CELLS, 256), stored[...].reshape(CELLS, 256)]
    for f, field in enumerate(fields):
        table[8 * f : 8 * f + 8, :] = cells_to_lanes(field)
    table[FLAGS:ROWS, :] = flags[...]
    faces[...] = picked(table[...], sent[0:1, :])


def doubled(rows, group):
    swapped = pltpu.roll(rows, 4, 0)
    low = lax.broadcasted_iota(i32, rows.shape, 0) < 4
    return jnp.where(low, rows, swapped) if group == 0 else jnp.where(low, swapped, rows)


def store_rows(target, feature, rows):
    for group in range(2):
        both = doubled(rows, group)
        for t in range(TILES):
            target[feature, group * TILES + t] = both[:, 128 * t : 128 * t + 128]


def store_columns(target, feature, block, natural):
    low = lax.broadcasted_iota(i32, (8, 128), 0) < 4
    for s in range(8):
        first = jnp.broadcast_to(natural[s : s + 1, :128], (8, 128))
        second = jnp.broadcast_to(natural[s : s + 1, 128:], (8, 128))
        target[block * 8 + s, feature] = jnp.where(low, first, second)


def build_lists(table, coord, list_d, list_f, count_d, count_f):
    active = lax.broadcasted_iota(i32, (8, LANES), 0).astype(f32) < table[LIVE : LIVE + 1, :]
    reach = 4.0 * table[32:40, :] * table[32:40, :] * 1.0001
    squares = []
    for c in range(3):
        p = table[8 * c : 8 * c + 8, :]
        squares.append({-1: p * p, 0: None, 1: (1.0 - p) * (1.0 - p)})
    far = jnp.where(active, 0.0, 1e9)
    cx, cy, cz = coord[0:1, :], coord[1:2, :], coord[2:3, :]
    entries_d, entries_f = [], []
    kept_d = kept_f = jnp.zeros((2, LANES), i32)
    center = 13
    offsets = OFFSETS[:center] + [(0, 0, 0)] + OFFSETS[center:]
    for k, (ox, oy, oz) in enumerate(offsets):
        away = far
        for c, o in enumerate((ox, oy, oz)):
            if o:
                away = away + squares[c][o]
        bx, by, bz = cx + ox, cy + oy, cz + oz
        ok = (bx >= 0) & (bx < BX) & (by >= 0) & (by < BY) & (bz >= 0) & (bz < BZ)
        if k != center:
            row = FLAGS + (k if k < center else k - 1)
            ok = ok & (table[row : row + 1, :] > 0.5)
        cell = (bx * BY + by) * BZ + bz
        over_d = away - reach
        over_f = away - 1.0001

        def near(over):
            return jnp.concatenate(
                [jnp.min(over[0:4], 0, keepdims=True), jnp.min(over[4:8], 0, keepdims=True)], 0
            )

        both = jnp.concatenate([cell, cell], 0)
        oks = jnp.concatenate([ok.astype(i32), ok.astype(i32)], 0) > 0
        for over, entries, which in ((over_d, entries_d, 0), (over_f, entries_f, 1)):
            keep = oks & (near(over) <= 0.0)
            kept = kept_d if which == 0 else kept_f
            entries.append(jnp.where(keep, both + (k - kept) * 1024, NONE))
            if which == 0:
                kept_d = kept + keep.astype(i32)
            else:
                kept_f = kept + keep.astype(i32)
    for entries, target, kept, counted in (
        (entries_d, list_d, kept_d, count_d), (entries_f, list_f, kept_f, count_f),
    ):
        for bit in range(5):
            step, mask = 1 << bit, 1024 << bit
            moves = [(e & mask) != 0 for e in entries]
            moved = []
            for p in range(27):
                e = jnp.where(moves[p], NONE, entries[p])
                if p + step < 27:
                    e = jnp.where(moves[p + step], entries[p + step], e)
                moved.append(e)
            entries = moved
        entries = [e & 1023 for e in entries] + [jnp.full((2, LANES), NONE, i32)]
        for p in range(28):
            for group in range(2):
                target[p : p + 1, group * LANES : group * LANES + LANES] = entries[p][group : group + 1]
        for group in range(2):
            counted[0:1, group * LANES : group * LANES + LANES] = kept[group : group + 1]


def work_items(counts, order):
    def step(i, carry):
        at, total = carry
        for u in range(16):
            group = i * 16 + u
            items = (counts[0, group] + SPAN - 1) // SPAN
            order[at] = group + items * 65536
            at = at + (items > 0).astype(i32)
            total = total + items
        return at, total

    at, total = lax.fori_loop(0, GROUPS // 16, step, (jnp.int32(0), jnp.int32(0)))
    order[at] = (GROUPS - 1) + (1 << 30)
    return total


def run_items(total, batch, order, lists, item):
    def advance(at, done):
        entry = order[at]
        last = done + 1 >= (entry >> 16)
        return (entry & 65535) + done * 65536, jnp.where(last, at + 1, at), jnp.where(last, 0, done + 1)

    def take(at, done):
        taken = []
        for _ in range(batch):
            code, at, done = advance(at, done)
            taken.append(code)
        return at, done, taken

    at, done, first = take(jnp.int32(0), jnp.int32(0))

    def step(_, carry):
        at, done, codes = carry
        at, done, later = take(at, done)
        for code in codes:
            group, part = code & 65535, code >> 16
            cells = [lists[part * SPAN + v, group] for v in range(SPAN)]
            item(group >> 7, group & 127, cells)
        return at, done, later

    lax.fori_loop(0, (total + batch - 1) // batch, step, (at, done, first))


def lane_of(lane):
    return jnp.full((8, 128), lane, i32)


def folded(partial_first, partial_second):
    low = lax.broadcasted_iota(i32, (8, 128), 0) < 4
    first = partial_first + pltpu.roll(partial_first, 4, 0)
    second = partial_second + pltpu.roll(partial_second, 4, 0)
    return jnp.where(low, first, second)


def density_kernel(
    parts, coord, source, pos, mass, count, table, list_f, count_f, sums,
    list_v, count_v, list_s, count_s, order, rows, columns, total, natural, sem,
):
    table[...] = picked(parts[...], source[0:1, :])
    build_lists(table, coord, list_v, list_f, count_v, count_f)
    first_copy = pltpu.make_async_copy(list_v, list_s, sem.at[0])
    second_copy = pltpu.make_async_copy(count_v, count_s, sem.at[1])
    first_copy.start()
    second_copy.start()
    place = coord[...].astype(f32)
    for c in range(3):
        store_rows(rows, c, table[8 * c : 8 * c + 8, :] + place[c : c + 1, :])
    smooth = table[32:40, :]
    home = lax.broadcasted_iota(i32, (8, LANES), 1) < EXT
    safe = jnp.where(home, smooth, 1.0)
    store_rows(rows, 3, 1.0 / safe)
    for c in range(3):
        natural[c] = pos[c].reshape(CELLS, 256)
    natural[3] = live_mass(mass[...].reshape(CELLS, 256), count[...])

    def fill(block, _):
        start = pl.ds(pl.multiple_of(block * 8, 8), 8)
        cell = block * 8 + lax.broadcasted_iota(i32, (8, 256), 0)
        for c, value in enumerate((cell // 16, (cell // 4) % 4, cell % 4)):
            store_columns(columns, c, block, natural[c, start, :] + value.astype(f32))
        store_columns(columns, 3, block, natural[3, start, :])
        return 0

    lax.fori_loop(0, CELLS // 8, fill, 0)
    columns[NONE] = jnp.zeros((4, 8, 128), f32)
    total[...] = jnp.zeros_like(total)
    first_copy.wait()
    second_copy.wait()
    lane_index = lax.broadcasted_iota(i32, (8, 128), 1)

    def item(tile, lane, cells):
        at = lane_of(lane)
        row = [jnp.take_along_axis(rows[f, tile], at, axis=1) for f in range(4)]
        acc = None
        for cell in cells:
            d = [row[c] - columns[cell, c] for c in range(3)]
            r2 = d[0] * d[0] + d[1] * d[1] + d[2] * d[2]
            r = r2 * lax.rsqrt(jnp.maximum(r2, 1e-30))
            u = jnp.maximum(2.0 - r * row[3], 0.0)
            v = jnp.maximum(u - 1.0, 0.0)
            term = columns[cell, 3] * (u * u * u - 4.0 * (v * v * v))
            acc = term if acc is None else acc + term
        summed = jnp.sum(acc, axis=1, keepdims=True)
        total[tile] = total[tile] + jnp.where(lane_index == lane, summed, 0.0)

    run_items(work_items(count_s, order), BATCH_D, order, list_s, item)
    scale = 1.0 / (4.0 * math.pi * safe * safe * safe)
    for t in range(TILES):
        both = folded(total[t], total[TILES + t])
        sums[:, 128 * t : 128 * t + 128] = both * scale[:, 128 * t : 128 * t + 128]


def home_lanes():
    cell = np.arange(CELLS)
    lane = ((cell // 16 + 1) * EY + (cell // 4) % 4 + 1) * EZ + cell % 4 + 1
    return np.tile(lane.astype(np.int32), (8, 1))


def state(entropy, density):
    pressure = entropy * jnp.exp(jnp.log(density) * (-1.0 / 3.0))
    return pressure, jnp.sqrt(ADIABATIC * pressure * density)


def force_kernel(
    table, fresh, list_s, count_s, coord, home, pos, vel, mass, smooth, entropy, stored, count,
    active, sums, density, order, rows, columns, total, natural,
):
    is_cell = lax.broadcasted_iota(i32, (8, LANES), 1) < EXT
    live = lax.broadcasted_iota(i32, (8, LANES), 0).astype(f32) < table[LIVE : LIVE + 1, :]
    place = coord[...].astype(f32)

    def field(f):
        return table[8 * f : 8 * f + 8, :]

    rho = jnp.where(is_cell, jnp.where(live, fresh[...], field(9)), 1.0)
    row_h = jnp.where(is_cell, field(4), 1.0)
    row_p, row_s = state(field(8), rho)

    def features(h, sound, dens, pressure):
        a = math.sqrt(0.75 / math.pi) / (h * h)
        return 2.0 * a, a / h, 0.05 * h, 0.5 * sound, 2.0 * dens, pressure

    for c in range(3):
        store_rows(rows, c, field(c) + place[c : c + 1, :])
        store_rows(rows, 3 + c, 20.0 * field(5 + c))
    for f, value in enumerate(features(row_h, row_s, rho, row_p)):
        store_rows(rows, 6 + f, value)

    slot = lax.broadcasted_iota(i32, (CELLS, 128), 1)
    updated = lanes_to_cells(picked(rho, home[0:1, :]))
    old = stored[...].reshape(CELLS, 256)
    new = jnp.concatenate([jnp.where(slot < active[...], updated, old[:, :128]), old[:, 128:]], 1)
    density[...] = new.reshape(BX, BY, BZ, 256)
    for c in range(3):
        natural[c] = pos[c].reshape(CELLS, 256)
        natural[3 + c] = vel[c].reshape(CELLS, 256)
    natural[6] = live_mass(mass[...].reshape(CELLS, 256), count[...])
    natural[7] = smooth[...].reshape(CELLS, 256)
    natural[8] = entropy[...].reshape(CELLS, 256)
    natural[9] = new

    def fill(block, _):
        start = pl.ds(pl.multiple_of(block * 8, 8), 8)
        cell = block * 8 + lax.broadcasted_iota(i32, (8, 256), 0)
        for c, value in enumerate((cell // 16, (cell // 4) % 4, cell % 4)):
            store_columns(columns, c, block, natural[c, start, :] + value.astype(f32))
            store_columns(columns, 3 + c, block, 20.0 * natural[3 + c, start, :])
        dens = natural[9, start, :]
        pressure, sound = state(natural[8, start, :], dens)
        for f, value in enumerate(features(natural[7, start, :], sound, dens, pressure)):
            store_columns(columns, 6 + f, block, value)
        store_columns(columns, 12, block, natural[6, start, :])
        return 0

    lax.fori_loop(0, CELLS // 8, fill, 0)
    columns[NONE] = jnp.ones((13, 8, 128), f32)
    columns[NONE, 12] = jnp.zeros((8, 128), f32)
    total[...] = jnp.zeros_like(total)
    lane_index = lax.broadcasted_iota(i32, (8, 128), 1)

    def item(tile, lane, cells):
        at = lane_of(lane)
        row = [jnp.take_along_axis(rows[f, tile], at, axis=1) for f in range(12)]
        acc = [None] * 3
        for cell in cells:
            col = [columns[cell, f] for f in range(13)]
            d = [row[c] - col[c] for c in range(3)]
            r2 = d[0] * d[0] + d[1] * d[1] + d[2] * d[2]
            closing = (
                (row[3] - col[3]) * d[0] + (row[4] - col[4]) * d[1] + (row[5] - col[5]) * d[2]
            )
            inverse = lax.rsqrt(jnp.maximum(r2, 1e-30))
            r = r2 * inverse

            def slope(twice, per):
                t = per * r
                u = jnp.maximum(twice - t, 0.0)
                s = jnp.minimum(t, u)
                return s * (u + (u - s))

            h = row[8] + col[8]
            approach = (h * jnp.minimum(closing, 0.0)) * pl.reciprocal(r2 + h * h, approx=True)
            viscosity = (approach * (approach - (row[9] + col[9]))) * pl.reciprocal(
                row[10] + col[10], approx=True
            )
            weight = (row[11] + viscosity) * slope(row[6], row[7])
            weight = weight + (col[11] + viscosity) * slope(col[6], col[7])
            weight = weight * (inverse * col[12])
            for c in range(3):
                term = weight * d[c]
                acc[c] = term if acc[c] is None else acc[c] + term
        mine = lane_index == lane
        for c in range(3):
            summed = jnp.sum(acc[c], axis=1, keepdims=True)
            total[c, tile] = total[c, tile] + jnp.where(mine, summed, 0.0)

    run_items(work_items(count_s, order), BATCH_F, order, list_s, item)
    for c in range(3):
        for t in range(TILES):
            sums[8 * c : 8 * c + 8, 128 * t : 128 * t + 128] = folded(total[c, t], total[c, TILES + t])


def spread_kernel(pushed, home, active, out):
    mine = picked(pushed[...], home[0:1, :])
    slot = lax.broadcasted_iota(i32, (CELLS, 128), 1)
    for c in range(3):
        rows = lanes_to_cells(mine[8 * c : 8 * c + 8, :])
        rows = jnp.where(slot < active[...], rows, 0.0)
        out[c] = jnp.concatenate([rows, jnp.zeros((CELLS, 128), f32)], 1).reshape(BX, BY, BZ, 256)


VMEM_SPEC = pl.BlockSpec(memory_space=pltpu.VMEM)
SMEM_SPEC = pl.BlockSpec(memory_space=pltpu.SMEM)
PARAMS = pltpu.CompilerParams(vmem_limit_bytes=56 * 1024 * 1024)


def shape(*dims, dtype=f32):
    return jax.ShapeDtypeStruct(dims, dtype)


def call(kernel, inputs, outputs, in_specs=None, scratch=()):
    single = not isinstance(outputs, (list, tuple))
    return pl.pallas_call(
        kernel,
        out_shape=outputs,
        in_specs=in_specs or [VMEM_SPEC] * len(inputs),
        out_specs=VMEM_SPEC if single else [VMEM_SPEC] * len(outputs),
        scratch_shapes=list(scratch),
        compiler_params=PARAMS,
    )(*inputs)


def ring(axis, by):
    devices = lax.axis_size(axis)
    return [(i, (i + by) % devices) for i in range(devices)]


def first_exchange(table, faces):
    y_part, z_part, edge = faces[:, :128], faces[:, 128:256], faces[:, 256:320]
    across = ("gy", "gz")
    y_in = lax.ppermute(y_part, across, [(0, 2), (1, 3), (2, 0), (3, 1)])
    z_in = lax.ppermute(z_part, across, [(0, 1), (1, 0), (2, 3), (3, 2)])
    edge_in = lax.ppermute(edge, across, [(0, 3), (1, 2), (2, 1), (3, 0)])
    low = jnp.concatenate([table[:, :16], y_in[:, :8], z_in[:, :8], edge_in[:, :4]], 1)
    high = jnp.concatenate([table[:, 240:], y_in[:, 120:], z_in[:, 120:], edge_in[:, 60:]], 1)
    before = lax.ppermute(high, "gx", ring("gx", 1))
    after = lax.ppermute(low, "gx", ring("gx", -1))
    unused = jnp.zeros((ROWS, LANES - EXT), f32)
    return jnp.concatenate([table, y_in, z_in, edge_in, before, after, unused], 1)


def turned(values, by):
    return jnp.concatenate([values[:, -by:], values[:, :-by]], 1) if by > 0 else jnp.concatenate(
        [values[:, -by:], values[:, :-by]], 1
    )


def shared_sums(sums, coord):
    plane = EY * EZ
    top = BX * plane
    before = lax.ppermute(sums[:, top : top + 2 * plane], "gx", ring("gx", 1))
    after = lax.ppermute(sums[:, : 2 * plane], "gx", ring("gx", -1))
    middle = sums[:, 2 * plane : top]
    sums = jnp.concatenate(
        [sums[:, : 2 * plane] + before, middle, sums[:, top:EXT] + after, sums[:, EXT:]], 1
    )
    for axis, step, position, extent in (("gy", EZ, coord[1:2], BY), ("gz", 1, coord[2:3], BZ)):
        other = lax.ppermute(sums, axis, ring(axis, 1))
        shift = extent * step
        low = (position == -1) | (position == 0)
        high = (position == extent - 1) | (position == extent)
        sums = sums + jnp.where(low, turned(other, -shift), jnp.where(high, turned(other, shift), 0.0))
    return sums


def returned_sums(sums, coord):
    plane = EY * EZ
    top = BX * plane
    before = lax.ppermute(sums[:, top + plane : EXT], "gx", ring("gx", 1))
    after = lax.ppermute(sums[:, :plane], "gx", ring("gx", -1))
    sums = jnp.concatenate(
        [
            sums[:, :plane],
            sums[:, plane : 2 * plane] + before,
            sums[:, 2 * plane : top],
            sums[:, top : top + plane] + after,
            sums[:, top + plane :],
        ],
        1,
    )
    for axis, step, position, extent in (("gy", EZ, coord[1:2], BY), ("gz", 1, coord[2:3], BZ)):
        other = lax.ppermute(sums, axis, ring(axis, 1))
        shift = extent * step
        sums = sums + jnp.where(
            position == 0,
            turned(other, -shift),
            jnp.where(position == extent - 1, turned(other, shift), 0.0),
        )
    return sums


def shards(pos, vel, mass, smooth, entropy, stored, particle_count, active_count, pair_side):
    coord_np, source_np = maps()
    coord, source = jnp.asarray(coord_np), jnp.asarray(source_np)
    home = jnp.asarray(home_lanes())
    count = particle_count.reshape(CELLS, 1)
    active = active_count.reshape(CELLS, 1)
    flags = jnp.concatenate(
        [
            pair_side.reshape(26, CELLS).astype(f32),
            active_count.reshape(1, CELLS).astype(f32),
            jnp.zeros((ROWS - FLAGS - 27, CELLS), f32),
        ],
        0,
    )
    inputs = (pos, vel, mass, smooth, entropy, stored, count, flags, jnp.asarray(sent_cells()))
    table, faces = call(pack_kernel, inputs, [shape(ROWS, CELLS), shape(ROWS, 384)])
    parts = first_exchange(table, faces)
    inputs = (parts, coord, source, pos, mass, count)
    table, list_f, count_f, sums = call(
        density_kernel,
        inputs,
        [
            shape(ROWS, LANES), shape(28, GROUPS, dtype=i32), shape(1, GROUPS, dtype=i32),
            shape(ACT, LANES),
        ],
        scratch=[
            pltpu.VMEM((28, GROUPS), i32), pltpu.VMEM((1, GROUPS), i32),
            pltpu.SMEM((28, GROUPS), i32), pltpu.SMEM((1, GROUPS), i32),
            pltpu.SMEM((GROUPS + 128,), i32), pltpu.VMEM((4, 2 * TILES, 8, 128), f32),
            pltpu.VMEM((CELLS + 1, 4, 8, 128), f32), pltpu.VMEM((2 * TILES, 8, 128), f32),
            pltpu.VMEM((4, CELLS, 256), f32), pltpu.SemaphoreType.DMA((2,)),
        ],
    )
    fresh = shared_sums(sums, coord)
    inputs = (
        table, fresh, list_f, count_f, coord, home, pos, vel, mass, smooth, entropy, stored,
        count, active,
    )
    sums, density = call(
        force_kernel,
        inputs,
        [shape(24, LANES), shape(BX, BY, BZ, 256)],
        in_specs=[VMEM_SPEC, VMEM_SPEC, SMEM_SPEC, SMEM_SPEC] + [VMEM_SPEC] * 10,
        scratch=[
            pltpu.SMEM((GROUPS + 128,), i32), pltpu.VMEM((12, 2 * TILES, 8, 128), f32),
            pltpu.VMEM((CELLS + 1, 13, 8, 128), f32), pltpu.VMEM((3, 2 * TILES, 8, 128), f32),
            pltpu.VMEM((10, CELLS, 256), f32),
        ],
    )
    pushed = returned_sums(sums, coord)
    acceleration = call(spread_kernel, (pushed, home, active), shape(3, BX, BY, BZ, 256))
    return density, acceleration


def solution(mesh):
    cells = P("gx", "gy", "gz", None)
    vectors = P(None, "gx", "gy", "gz", None)
    counts = P("gx", "gy", "gz")
    in_specs = (
        vectors, vectors, cells, cells, cells, cells, counts, counts, P(None, "gx", "gy", "gz"),
    )
    return jax.shard_map(
        shards, mesh=mesh, in_specs=in_specs, out_specs=(cells, vectors), check_vma=False
    )
```

```python
import functools
import math

import jax
import jax.numpy as jnp
import numpy as np
from jax import lax
from jax.experimental import pallas as pl
from jax.experimental.pallas import tpu as pltpu
from jax.sharding import PartitionSpec as P

ACT = 8
BX, BY, BZ = 16, 4, 4
CELLS = BX * BY * BZ
EX, EY, EZ = BX + 2, BY + 2, BZ + 2
EXT = EX * EY * EZ
LANES = 768
TILES = LANES // 128
GROUPS = 2 * LANES
ROWS = 112
FLAGS = 80
LIVE = 106
SPAN = 3
WORDS = 9
ITEM_ROWS = 96
LIST_ROWS = 112
HELD = 16
BATCH_D = 8
BATCH_F = 4
NONE = CELLS
ADIABATIC = 5.0 / 3.0
HIGHEST = lax.Precision.HIGHEST
f32 = jnp.float32
i32 = jnp.int32

OFFSETS = [
    (a, b, c) for a in (-1, 0, 1) for b in (-1, 0, 1) for c in (-1, 0, 1) if (a, b, c) != (0, 0, 0)
]


def maps():
    coord = np.full((8, LANES), -9, np.int32)
    coord[:3] = -5
    source = np.full((8, LANES), -1, np.int32)
    for x in range(-1, BX + 1):
        for y in range(-1, BY + 1):
            for z in range(-1, BZ + 1):
                lane = ((x + 1) * EY + y + 1) * EZ + z + 1
                coord[0, lane], coord[1, lane], coord[2, lane] = x, y, z
                inside_y, inside_z = 0 <= y < BY, 0 <= z < BZ
                face_y = 0 if y == BY else 1
                face_z = 0 if z == BZ else 1
                def place(width_home, width_y, width_z, width_yz, starts, row):
                    if inside_y and inside_z:
                        return starts[0] + row * width_home + y * BZ + z
                    if inside_z:
                        return starts[1] + row * width_y + face_y * BZ + z
                    if inside_y:
                        return starts[2] + row * width_z + y * 2 + face_z
                    return starts[3] + row * width_yz + face_y * 2 + face_z

                if 0 <= x < BX:
                    at = place(16, 8, 8, 4, (0, 256, 384, 512), x)
                else:
                    base = 576 if x < 0 else 612
                    at = place(16, 8, 8, 4, (base, base + 16, base + 24, base + 32), 0)
                source[0, lane] = at
    return coord, source


def sent_cells():
    table = np.full((8, 384), -1, np.int32)
    for x in range(BX):
        for face in range(2):
            for z in range(BZ):
                table[0, x * 8 + face * BZ + z] = (x * BY + (0 if face == 0 else BY - 1)) * BZ + z
            for y in range(BY):
                table[0, 128 + x * 8 + y * 2 + face] = (x * BY + y) * BZ + (
                    0 if face == 0 else BZ - 1
                )
            for other in range(2):
                table[0, 256 + x * 4 + face * 2 + other] = (
                    x * BY + (0 if face == 0 else BY - 1)
                ) * BZ + (0 if other == 0 else BZ - 1)
    return table


def picked(values, source_row):
    size = values.shape[1]
    rows = lax.broadcasted_iota(i32, (size, source_row.shape[1]), 0)
    chosen = (rows == source_row).astype(f32)
    return lax.dot_general(
        values, chosen, (((1,), (0,)), ((), ())), precision=HIGHEST, preferred_element_type=f32
    )


def unit_rows():
    return (
        lax.broadcasted_iota(i32, (ACT, 128), 0) == lax.broadcasted_iota(i32, (ACT, 128), 1)
    ).astype(f32)


def cells_to_lanes(natural):
    return lax.dot_general(
        unit_rows(), natural[:, :128], (((1,), (1,)), ((), ())), precision=HIGHEST,
        preferred_element_type=f32,
    )


def lanes_to_cells(rows):
    return lax.dot_general(
        rows, unit_rows(), (((0,), (0,)), ((), ())), precision=HIGHEST, preferred_element_type=f32
    )


def live_mass(mass, count):
    slot = lax.broadcasted_iota(i32, (CELLS, 256), 1)
    return jnp.where(slot < count, mass, 0.0)


def pack_kernel(pos, vel, mass, smooth, entropy, stored, count, flags, sent, table, faces):
    fields = [pos[c].reshape(CELLS, 256) for c in range(3)]
    fields.append(live_mass(mass[...].reshape(CELLS, 256), count[...]))
    fields.append(smooth[...].reshape(CELLS, 256))
    fields += [vel[c].reshape(CELLS, 256) for c in range(3)]
    fields += [entropy[...].reshape(CELLS, 256), stored[...].reshape(CELLS, 256)]
    for f, field in enumerate(fields):
        table[8 * f : 8 * f + 8, :] = cells_to_lanes(field)
    table[FLAGS:ROWS, :] = flags[...]
    faces[...] = picked(table[...], sent[0:1, :])


def segment_units():
    row = lax.broadcasted_iota(i32, (24, 256), 0) % 8
    lane = lax.broadcasted_iota(i32, (24, 256), 1)
    return (row == lane // 128 * 4 + lane % 128 // 32).astype(f32)


def store_rows(target, feature, rows):
    high = rows.astype(jnp.bfloat16).astype(f32)
    rest = rows - high
    middle = rest.astype(jnp.bfloat16).astype(f32)
    parts = jnp.concatenate([high, middle, rest - middle], 0)
    spread = lax.dot_general(
        parts, segment_units(), (((0,), (0,)), ((), ())), preferred_element_type=f32
    )
    for group in range(2):
        for block in range(LANES // 8):
            at = (group * LANES + block * 8) * HELD + feature
            target[pl.ds(at, 8, stride=HELD), :] = spread[
                8 * block : 8 * block + 8, 128 * group : 128 * group + 128
            ]


def store_columns(target, feature, block, count, natural):
    part = lax.broadcasted_iota(i32, (8, 128), 1) // 32
    for half in range(2):
        slots = natural[:, 128 * half : 128 * half + 128]
        turns = [slots] + [pltpu.roll(slots, 32 * t, 1) for t in range(1, 4)]
        for k in range(4):
            value = turns[(0 - k) % 4]
            for r in range(1, 4):
                value = jnp.where(part == r, turns[(r - k) % 4], value)
            at = (block * 8 * count + feature) * 8 + half * 4 + k
            target.reshape((CELLS + 1) * count * 8, 128)[pl.ds(at, 8, stride=count * 8), :] = value


def build_lists(table, coord, list_d, list_f, count_d, count_f):
    active = lax.broadcasted_iota(i32, (8, LANES), 0).astype(f32) < table[LIVE : LIVE + 1, :]
    reach = 4.0 * table[32:40, :] * table[32:40, :] * 1.0001
    squares = []
    for c in range(3):
        p = table[8 * c : 8 * c + 8, :]
        squares.append({-1: p * p, 0: None, 1: (1.0 - p) * (1.0 - p)})
    far = jnp.where(active, 0.0, 1e9)
    cx, cy, cz = coord[0:1, :], coord[1:2, :], coord[2:3, :]
    entries_d, entries_f = [], []
    kept_d = kept_f = jnp.zeros((2, LANES), i32)
    center = 13
    offsets = OFFSETS[:center] + [(0, 0, 0)] + OFFSETS[center:]
    for k, (ox, oy, oz) in enumerate(offsets):
        away = far
        for c, o in enumerate((ox, oy, oz)):
            if o:
                away = away + squares[c][o]
        bx, by, bz = cx + ox, cy + oy, cz + oz
        ok = (bx >= 0) & (bx < BX) & (by >= 0) & (by < BY) & (bz >= 0) & (bz < BZ)
        if k != center:
            row = FLAGS + (k if k < center else k - 1)
            ok = ok & (table[row : row + 1, :] > 0.5)
        cell = (bx * BY + by) * BZ + bz
        over_d = away - reach
        over_f = away - 1.0001

        def near(over):
            return jnp.concatenate(
                [jnp.min(over[0:4], 0, keepdims=True), jnp.min(over[4:8], 0, keepdims=True)], 0
            )

        both = jnp.concatenate([cell, cell], 0)
        oks = jnp.concatenate([ok.astype(i32), ok.astype(i32)], 0) > 0
        for over, entries, which in ((over_d, entries_d, 0), (over_f, entries_f, 1)):
            keep = oks & (near(over) <= 0.0)
            kept = kept_d if which == 0 else kept_f
            entries.append(jnp.where(keep, both + (k - kept) * 1024, NONE))
            if which == 0:
                kept_d = kept + keep.astype(i32)
            else:
                kept_f = kept + keep.astype(i32)
    for entries, target, kept, counted in (
        (entries_d, list_d, kept_d, count_d), (entries_f, list_f, kept_f, count_f),
    ):
        for bit in range(5):
            step, mask = 1 << bit, 1024 << bit
            moves = [(e & mask) != 0 for e in entries]
            moved = []
            for p in range(27):
                e = jnp.where(moves[p], NONE, entries[p])
                if p + step < 27:
                    e = jnp.where(moves[p + step], entries[p + step], e)
                moved.append(e)
            entries = moved
        entries = [e & 1023 for e in entries]
        for p in range(WORDS):
            word = entries[3 * p] + (entries[3 * p + 1] << 10) + (entries[3 * p + 2] << 20)
            for group in range(2):
                for t in range(TILES):
                    at = (p * 2 + group) * TILES + t
                    target[at : at + 1, :] = word[group : group + 1, 128 * t : 128 * t + 128]
        target[WORDS * 2 * TILES :, :] = jnp.full((LIST_ROWS - WORDS * 2 * TILES, 128), NONE, i32)
        for group in range(2):
            for t in range(TILES):
                counted[group * TILES + t : group * TILES + t + 1, :] = kept[
                    group : group + 1, 128 * t : 128 * t + 128
                ]
        counted[2 * TILES :, :] = jnp.zeros((16 - 2 * TILES, 128), i32)


def work_items(counts, items_v, items_s, ends, ends_v, ends_s, sem):
    items = jnp.floor((counts[...] + SPAN - 1).astype(f32) * (1.00002 / SPAN))
    row = lax.broadcasted_iota(i32, (128, 128), 0)
    lane = lax.broadcasted_iota(i32, (128, 128), 1)
    within = jnp.dot(items, (row <= lane).astype(f32), preferred_element_type=f32)
    whole = jnp.broadcast_to(within[:, 127:128], (16, 128))
    earlier = (
        lax.broadcasted_iota(i32, (16, 16), 1) < lax.broadcasted_iota(i32, (16, 16), 0)
    ).astype(f32)
    end = within + jnp.dot(earlier, whole, precision=HIGHEST, preferred_element_type=f32)
    ends_v[...] = end
    copy = pltpu.make_async_copy(ends_v, ends_s, sem)
    copy.start()
    for t in range(2 * TILES):
        ends[128 * t : 128 * t + 128, :] = jnp.broadcast_to(end[t : t + 1, :], (128, 128)).T
    items_v[...] = jnp.full((ITEM_ROWS, 128), (GROUPS - 1) * 2049, i32)
    copy.wait()
    last = [ends_s[t, 127].astype(i32) for t in range(2 * TILES)]
    total = last[-1]
    lanes = lax.broadcasted_iota(i32, (8, 128), 1)

    def fill(j, _):
        first = j * 128
        index = first + lanes
        number = index.astype(f32)
        begin = jnp.int32(0)
        stop = jnp.int32(0)
        before = jnp.int32(0)
        for e in last:
            begin = begin + (e <= first).astype(i32)
            stop = stop + (e <= first + 127).astype(i32)
            before = jnp.where(e <= first, e, before)
        stop = jnp.minimum(stop + 1, 2 * TILES)

        def tile(t, carry):
            passed, start = carry
            for u in range(16):
                e = ends[pl.ds(pl.multiple_of(t * 128 + u * 8, 8), 8), :]
                over = e <= number
                passed = passed + jnp.where(over, 1.0, 0.0)
                start = jnp.maximum(start, jnp.where(over, e, 0.0))
            return passed, start

        zero = jnp.zeros((8, 128), f32)
        passed, start = lax.fori_loop(begin, stop, tile, (zero, zero))
        group = begin * 128 + jnp.sum(passed, 0, keepdims=True).astype(i32)
        start = jnp.maximum(jnp.max(start, 0, keepdims=True).astype(i32), before)
        code = group + ((index[0:1] - start) * GROUPS + group) * 2048
        items_v[pl.ds(j, 1), :] = jnp.where(index[0:1] < total, code, (GROUPS - 1) * 2049)
        return 0

    lax.fori_loop(0, (total + 127) >> 7, fill, 0)
    copy = pltpu.make_async_copy(items_v, items_s, sem)
    copy.start()
    copy.wait()
    return total


def run_items(total, batch, items, lists, item, add):
    per_row = 128 // batch

    def take(turn):
        codes = [items[turn // per_row, (turn % per_row) * batch + u] for u in range(batch)]
        return codes, [lists[code >> 18, (code >> 11) & 127] for code in codes]

    def step(turn, carry):
        codes, words = carry
        later = take(turn + 1)
        results = []
        for code, word in zip(codes, words):
            group = code & 2047
            results.append((group, item(group, (word & 1023, (word >> 10) & 1023, word >> 20))))
        for group, values in results:
            add(group, values)
        return later

    lax.fori_loop(0, (total + batch - 1) // batch, step, take(jnp.int32(0)))


def row_sums(tiles, part_index, count, reduced):
    def block(i, _):
        for u in range(4):
            value = None
            for s in range(8):
                at = ((i * 32 + u * 8) * count + part_index) * 8 + s
                part = tiles.reshape(GROUPS * count * 8, 128)[pl.ds(at, 8, stride=8 * count), :]
                value = part if value is None else value + part
            reduced[pl.ds(pl.multiple_of(i * 32 + u * 8, 8), 8), :] = value
        return 0

    lax.fori_loop(0, GROUPS // 32, block, 0)
    row = lax.broadcasted_iota(i32, (8, 128), 0)
    segment = lax.broadcasted_iota(i32, (8, 128), 1) // 32
    out = None
    for group in range(2):
        values = reduced[LANES * group : LANES * group + LANES, :]
        unit = (row == segment + 4 * group).astype(f32)
        high = values.astype(jnp.bfloat16).astype(f32)
        for part in (high, values - high):
            term = lax.dot_general(
                unit, part, (((1,), (1,)), ((), ())), preferred_element_type=f32
            )
            out = term if out is None else out + term
    return out


def density_kernel(
    parts, coord, source, pos, mass, count, table, list_f, count_f, sums,
    list_v, count_v, list_s, items_v, items_s, ends, ends_v, ends_s, rows, columns, total, reduced,
    natural, sem,
):
    table[...] = picked(parts[...], source[0:1, :])
    build_lists(table, coord, list_v, list_f, count_v, count_f)
    list_copy = pltpu.make_async_copy(list_v, list_s, sem.at[0])
    list_copy.start()
    place = coord[...].astype(f32)
    for c in range(3):
        store_rows(rows, c, table[8 * c : 8 * c + 8, :] + place[c : c + 1, :])
    smooth = table[32:40, :]
    home = lax.broadcasted_iota(i32, (8, LANES), 1) < EXT
    safe = jnp.where(home, smooth, 1.0)
    store_rows(rows, 3, 1.0 / safe)
    for c in range(3):
        natural[c] = pos[c].reshape(CELLS, 256)
    natural[3] = live_mass(mass[...].reshape(CELLS, 256), count[...])

    def fill(block, _):
        start = pl.ds(pl.multiple_of(block * 8, 8), 8)
        cell = block * 8 + lax.broadcasted_iota(i32, (8, 256), 0)
        for c, value in enumerate((cell // 16, (cell // 4) % 4, cell % 4)):
            store_columns(columns, c, block, 4, natural[c, start, :] + value.astype(f32))
        store_columns(columns, 3, block, 4, natural[3, start, :])
        return 0

    lax.fori_loop(0, CELLS // 8, fill, 0)
    columns[NONE] = jnp.zeros((4, 8, 128), f32)
    total[...] = jnp.zeros_like(total)
    list_copy.wait()

    def item(group, cells):
        row = [rows[pl.ds(group * HELD + f, 8, stride=0), :] for f in range(4)]
        acc = None
        for cell in cells:
            col = [columns[cell, f] for f in range(4)]
            d = [row[c] - col[c] for c in range(3)]
            r2 = d[0] * d[0] + d[1] * d[1] + d[2] * d[2]
            r = r2 * lax.rsqrt(jnp.maximum(r2, 1e-30))
            u = jnp.maximum(2.0 - r * row[3], 0.0)
            v = jnp.maximum(u - 1.0, 0.0)
            term = col[3] * (u * u * u - 4.0 * (v * v * v))
            acc = term if acc is None else acc + term
        return acc

    def add(group, value):
        total[group, 0] = total[group, 0] + value

    number = work_items(count_v, items_v, items_s, ends, ends_v, ends_s, sem.at[1])
    run_items(number, BATCH_D, items_s, list_s, item, add)
    scale = 1.0 / (4.0 * math.pi * safe * safe * safe)
    sums[...] = row_sums(total, 0, 1, reduced) * scale


def home_lanes():
    cell = np.arange(CELLS)
    lane = ((cell // 16 + 1) * EY + (cell // 4) % 4 + 1) * EZ + cell % 4 + 1
    return np.tile(lane.astype(np.int32), (8, 1))


def state(entropy, density):
    pressure = entropy * jnp.exp(jnp.log(density) * (-1.0 / 3.0))
    return pressure, jnp.sqrt(ADIABATIC * pressure * density)


def force_kernel(
    table, fresh, list_v, count_v, coord, home, pos, vel, mass, smooth, entropy, stored, count,
    active, sums, density, list_s, items_v, items_s, ends, ends_v, ends_s, rows, columns, total, reduced,
    natural, sem,
):
    list_copy = pltpu.make_async_copy(list_v, list_s, sem.at[0])
    list_copy.start()
    is_cell = lax.broadcasted_iota(i32, (8, LANES), 1) < EXT
    live = lax.broadcasted_iota(i32, (8, LANES), 0).astype(f32) < table[LIVE : LIVE + 1, :]
    place = coord[...].astype(f32)

    def field(f):
        return table[8 * f : 8 * f + 8, :]

    rho = jnp.where(is_cell, jnp.where(live, fresh[...], field(9)), 1.0)
    row_h = jnp.where(is_cell, field(4), 1.0)
    row_p, row_s = state(field(8), rho)

    def features(h, sound, dens, pressure):
        a = math.sqrt(0.75 / math.pi) / (h * h)
        return 2.0 * a, a / h, 0.05 * h, 0.5 * sound, 2.0 * dens, pressure

    for c in range(3):
        store_rows(rows, c, field(c) + place[c : c + 1, :])
        store_rows(rows, 3 + c, 20.0 * field(5 + c))
    for f, value in enumerate(features(row_h, row_s, rho, row_p)):
        store_rows(rows, 6 + f, value)

    slot = lax.broadcasted_iota(i32, (CELLS, 128), 1)
    updated = lanes_to_cells(picked(rho, home[0:1, :]))
    old = stored[...].reshape(CELLS, 256)
    new = jnp.concatenate([jnp.where(slot < active[...], updated, old[:, :128]), old[:, 128:]], 1)
    density[...] = new.reshape(BX, BY, BZ, 256)
    for c in range(3):
        natural[c] = pos[c].reshape(CELLS, 256)
        natural[3 + c] = vel[c].reshape(CELLS, 256)
    natural[6] = live_mass(mass[...].reshape(CELLS, 256), count[...])
    natural[7] = smooth[...].reshape(CELLS, 256)
    natural[8] = entropy[...].reshape(CELLS, 256)
    natural[9] = new

    def fill(block, _):
        start = pl.ds(pl.multiple_of(block * 8, 8), 8)
        cell = block * 8 + lax.broadcasted_iota(i32, (8, 256), 0)
        for c, value in enumerate((cell // 16, (cell // 4) % 4, cell % 4)):
            store_columns(columns, c, block, 13, natural[c, start, :] + value.astype(f32))
            store_columns(columns, 3 + c, block, 13, 20.0 * natural[3 + c, start, :])
        dens = natural[9, start, :]
        pressure, sound = state(natural[8, start, :], dens)
        for f, value in enumerate(features(natural[7, start, :], sound, dens, pressure)):
            store_columns(columns, 6 + f, block, 13, value)
        store_columns(columns, 12, block, 13, natural[6, start, :])
        return 0

    lax.fori_loop(0, CELLS // 8, fill, 0)
    columns[NONE] = jnp.ones((13, 8, 128), f32)
    columns[NONE, 12] = jnp.zeros((8, 128), f32)
    total[...] = jnp.zeros_like(total)
    list_copy.wait()

    def item(group, cells):
        row = [rows[pl.ds(group * HELD + f, 8, stride=0), :] for f in range(12)]
        acc = [None] * 3
        for cell in cells:
            col = [columns[cell, f] for f in range(13)]
            d = [row[c] - col[c] for c in range(3)]
            r2 = d[0] * d[0] + d[1] * d[1] + d[2] * d[2]
            closing = (
                (row[3] - col[3]) * d[0] + (row[4] - col[4]) * d[1] + (row[5] - col[5]) * d[2]
            )
            inverse = lax.rsqrt(jnp.maximum(r2, 1e-30))
            r = r2 * inverse

            def slope(twice, per):
                t = per * r
                u = jnp.maximum(twice - t, 0.0)
                s = jnp.minimum(t, u)
                return s * (u + (u - s))

            h = row[8] + col[8]
            approach = (h * jnp.minimum(closing, 0.0)) * pl.reciprocal(r2 + h * h, approx=True)
            viscosity = (approach * (approach - (row[9] + col[9]))) * pl.reciprocal(
                row[10] + col[10], approx=True
            )
            weight = (row[11] + viscosity) * slope(row[6], row[7])
            weight = weight + (col[11] + viscosity) * slope(col[6], col[7])
            weight = weight * (inverse * col[12])
            for c in range(3):
                term = weight * d[c]
                acc[c] = term if acc[c] is None else acc[c] + term
        return acc

    def add(group, values):
        for c in range(3):
            total[group, c] = total[group, c] + values[c]

    number = work_items(count_v, items_v, items_s, ends, ends_v, ends_s, sem.at[1])
    run_items(number, BATCH_F, items_s, list_s, item, add)
    for c in range(3):
        sums[8 * c : 8 * c + 8, :] = row_sums(total, c, 3, reduced)


def spread_kernel(pushed, home, active, out):
    mine = picked(pushed[...], home[0:1, :])
    slot = lax.broadcasted_iota(i32, (CELLS, 128), 1)
    for c in range(3):
        rows = lanes_to_cells(mine[8 * c : 8 * c + 8, :])
        rows = jnp.where(slot < active[...], rows, 0.0)
        out[c] = jnp.concatenate([rows, jnp.zeros((CELLS, 128), f32)], 1).reshape(BX, BY, BZ, 256)


VMEM_SPEC = pl.BlockSpec(memory_space=pltpu.VMEM)
SMEM_SPEC = pl.BlockSpec(memory_space=pltpu.SMEM)
PARAMS = pltpu.CompilerParams(vmem_limit_bytes=56 * 1024 * 1024)


def shape(*dims, dtype=f32):
    return jax.ShapeDtypeStruct(dims, dtype)


def call(kernel, inputs, outputs, in_specs=None, scratch=()):
    single = not isinstance(outputs, (list, tuple))
    return pl.pallas_call(
        kernel,
        out_shape=outputs,
        in_specs=in_specs or [VMEM_SPEC] * len(inputs),
        out_specs=VMEM_SPEC if single else [VMEM_SPEC] * len(outputs),
        scratch_shapes=list(scratch),
        compiler_params=PARAMS,
    )(*inputs)


def item_scratch():
    return [
        pltpu.VMEM((ITEM_ROWS, 128), i32), pltpu.SMEM((ITEM_ROWS, 128), i32),
        pltpu.VMEM((GROUPS, 128), f32), pltpu.VMEM((16, 128), f32), pltpu.SMEM((16, 128), f32),
    ]


def density_scratch():
    return [
        pltpu.VMEM((LIST_ROWS, 128), i32), pltpu.VMEM((16, 128), i32), pltpu.SMEM((LIST_ROWS, 128), i32),
        *item_scratch(), pltpu.VMEM((GROUPS * HELD, 128), f32), pltpu.VMEM((CELLS + 1, 4, 8, 128), f32),
        pltpu.VMEM((GROUPS, 1, 8, 128), f32), pltpu.VMEM((GROUPS, 128), f32),
        pltpu.VMEM((4, CELLS, 256), f32), pltpu.SemaphoreType.DMA((2,)),
    ]


def force_scratch():
    return [
        pltpu.SMEM((LIST_ROWS, 128), i32), *item_scratch(), pltpu.VMEM((GROUPS * HELD, 128), f32), pltpu.VMEM((CELLS + 1, 13, 8, 128), f32),
        pltpu.VMEM((GROUPS, 3, 8, 128), f32), pltpu.VMEM((GROUPS, 128), f32),
        pltpu.VMEM((10, CELLS, 256), f32), pltpu.SemaphoreType.DMA((2,)),
    ]


def ring(axis, by):
    devices = lax.axis_size(axis)
    return [(i, (i + by) % devices) for i in range(devices)]


def first_exchange(table, faces):
    y_part, z_part, edge = faces[:, :128], faces[:, 128:256], faces[:, 256:320]
    across = ("gy", "gz")
    y_in = lax.ppermute(y_part, across, [(0, 2), (1, 3), (2, 0), (3, 1)])
    z_in = lax.ppermute(z_part, across, [(0, 1), (1, 0), (2, 3), (3, 2)])
    edge_in = lax.ppermute(edge, across, [(0, 3), (1, 2), (2, 1), (3, 0)])
    low = jnp.concatenate([table[:, :16], y_in[:, :8], z_in[:, :8], edge_in[:, :4]], 1)
    high = jnp.concatenate([table[:, 240:], y_in[:, 120:], z_in[:, 120:], edge_in[:, 60:]], 1)
    before = lax.ppermute(high, "gx", ring("gx", 1))
    after = lax.ppermute(low, "gx", ring("gx", -1))
    unused = jnp.zeros((ROWS, LANES - EXT), f32)
    return jnp.concatenate([table, y_in, z_in, edge_in, before, after, unused], 1)


def turned(values, by):
    return jnp.concatenate([values[:, -by:], values[:, :-by]], 1) if by > 0 else jnp.concatenate(
        [values[:, -by:], values[:, :-by]], 1
    )


def shared_sums(sums, coord):
    plane = EY * EZ
    top = BX * plane
    before = lax.ppermute(sums[:, top : top + 2 * plane], "gx", ring("gx", 1))
    after = lax.ppermute(sums[:, : 2 * plane], "gx", ring("gx", -1))
    middle = sums[:, 2 * plane : top]
    sums = jnp.concatenate(
        [sums[:, : 2 * plane] + before, middle, sums[:, top:EXT] + after, sums[:, EXT:]], 1
    )
    for axis, step, position, extent in (("gy", EZ, coord[1:2], BY), ("gz", 1, coord[2:3], BZ)):
        other = lax.ppermute(sums, axis, ring(axis, 1))
        shift = extent * step
        low = (position == -1) | (position == 0)
        high = (position == extent - 1) | (position == extent)
        sums = sums + jnp.where(low, turned(other, -shift), jnp.where(high, turned(other, shift), 0.0))
    return sums


def returned_sums(sums, coord):
    plane = EY * EZ
    top = BX * plane
    before = lax.ppermute(sums[:, top + plane : EXT], "gx", ring("gx", 1))
    after = lax.ppermute(sums[:, :plane], "gx", ring("gx", -1))
    sums = jnp.concatenate(
        [
            sums[:, :plane],
            sums[:, plane : 2 * plane] + before,
            sums[:, 2 * plane : top],
            sums[:, top : top + plane] + after,
            sums[:, top + plane :],
        ],
        1,
    )
    for axis, step, position, extent in (("gy", EZ, coord[1:2], BY), ("gz", 1, coord[2:3], BZ)):
        other = lax.ppermute(sums, axis, ring(axis, 1))
        shift = extent * step
        sums = sums + jnp.where(
            position == 0,
            turned(other, -shift),
            jnp.where(position == extent - 1, turned(other, shift), 0.0),
        )
    return sums


def shards(pos, vel, mass, smooth, entropy, stored, particle_count, active_count, pair_side):
    coord_np, source_np = maps()
    coord, source = jnp.asarray(coord_np), jnp.asarray(source_np)
    home = jnp.asarray(home_lanes())
    count = particle_count.reshape(CELLS, 1)
    active = active_count.reshape(CELLS, 1)
    flags = jnp.concatenate(
        [
            pair_side.reshape(26, CELLS).astype(f32),
            active_count.reshape(1, CELLS).astype(f32),
            jnp.zeros((ROWS - FLAGS - 27, CELLS), f32),
        ],
        0,
    )
    inputs = (pos, vel, mass, smooth, entropy, stored, count, flags, jnp.asarray(sent_cells()))
    table, faces = call(pack_kernel, inputs, [shape(ROWS, CELLS), shape(ROWS, 384)])
    parts = first_exchange(table, faces)
    inputs = (parts, coord, source, pos, mass, count)
    table, list_f, count_f, sums = call(
        density_kernel,
        inputs,
        [
            shape(ROWS, LANES), shape(LIST_ROWS, 128, dtype=i32), shape(16, 128, dtype=i32),
            shape(ACT, LANES),
        ],
        scratch=density_scratch(),
    )
    fresh = shared_sums(sums, coord)
    inputs = (
        table, fresh, list_f, count_f, coord, home, pos, vel, mass, smooth, entropy, stored,
        count, active,
    )
    sums, density = call(
        force_kernel,
        inputs,
        [shape(24, LANES), shape(BX, BY, BZ, 256)],

        scratch=force_scratch(),
    )
    pushed = returned_sums(sums, coord)
    acceleration = call(spread_kernel, (pushed, home, active), shape(3, BX, BY, BZ, 256))
    return density, acceleration


def solution(mesh):
    cells = P("gx", "gy", "gz", None)
    vectors = P(None, "gx", "gy", "gz", None)
    counts = P("gx", "gy", "gz")
    in_specs = (
        vectors, vectors, cells, cells, cells, cells, counts, counts, P(None, "gx", "gy", "gz"),
    )
    return jax.shard_map(
        shards, mesh=mesh, in_specs=in_specs, out_specs=(cells, vectors), check_vma=False
    )
```

```python
import functools
import math

import jax
import jax.numpy as jnp
import numpy as np
from jax import lax
from jax.experimental import pallas as pl
from jax.experimental.pallas import tpu as pltpu
from jax.sharding import PartitionSpec as P

ACT = 8
BX, BY, BZ = 16, 4, 4
CELLS = BX * BY * BZ
EX, EY, EZ = BX + 2, BY + 2, BZ + 2
EXT = EX * EY * EZ
LANES = 768
TILES = LANES // 128
GROUPS = 2 * LANES
ROWS = 112
FLAGS = 80
LIVE = 106
SPAN = 3
WORDS = 9
ITEM_ROWS = 96
LIST_ROWS = 112
HELD = 13
BATCH_D = 8
BATCH_F = 8
NONE = CELLS
ADIABATIC = 5.0 / 3.0
HIGHEST = lax.Precision.HIGHEST
f32 = jnp.float32
i32 = jnp.int32

OFFSETS = [
    (a, b, c) for a in (-1, 0, 1) for b in (-1, 0, 1) for c in (-1, 0, 1) if (a, b, c) != (0, 0, 0)
]


def maps():
    coord = np.full((8, LANES), -9, np.int32)
    coord[:3] = -5
    source = np.full((8, LANES), -1, np.int32)
    for x in range(-1, BX + 1):
        for y in range(-1, BY + 1):
            for z in range(-1, BZ + 1):
                lane = ((x + 1) * EY + y + 1) * EZ + z + 1
                coord[0, lane], coord[1, lane], coord[2, lane] = x, y, z
                inside_y, inside_z = 0 <= y < BY, 0 <= z < BZ
                face_y = 0 if y == BY else 1
                face_z = 0 if z == BZ else 1
                def place(width_home, width_y, width_z, width_yz, starts, row):
                    if inside_y and inside_z:
                        return starts[0] + row * width_home + y * BZ + z
                    if inside_z:
                        return starts[1] + row * width_y + face_y * BZ + z
                    if inside_y:
                        return starts[2] + row * width_z + y * 2 + face_z
                    return starts[3] + row * width_yz + face_y * 2 + face_z

                if 0 <= x < BX:
                    at = place(16, 8, 8, 4, (0, 256, 384, 512), x)
                else:
                    base = 576 if x < 0 else 612
                    at = place(16, 8, 8, 4, (base, base + 16, base + 24, base + 32), 0)
                source[0, lane] = at
    return coord, source


def sent_cells():
    table = np.full((8, 384), -1, np.int32)
    for x in range(BX):
        for face in range(2):
            for z in range(BZ):
                table[0, x * 8 + face * BZ + z] = (x * BY + (0 if face == 0 else BY - 1)) * BZ + z
            for y in range(BY):
                table[0, 128 + x * 8 + y * 2 + face] = (x * BY + y) * BZ + (
                    0 if face == 0 else BZ - 1
                )
            for other in range(2):
                table[0, 256 + x * 4 + face * 2 + other] = (
                    x * BY + (0 if face == 0 else BY - 1)
                ) * BZ + (0 if other == 0 else BZ - 1)
    return table


def picked(values, source_row):
    size = values.shape[1]
    rows = lax.broadcasted_iota(i32, (size, source_row.shape[1]), 0)
    chosen = (rows == source_row).astype(f32)
    return lax.dot_general(
        values, chosen, (((1,), (0,)), ((), ())), precision=HIGHEST, preferred_element_type=f32
    )


def unit_rows():
    return (
        lax.broadcasted_iota(i32, (ACT, 128), 0) == lax.broadcasted_iota(i32, (ACT, 128), 1)
    ).astype(f32)


def cells_to_lanes(natural):
    return lax.dot_general(
        unit_rows(), natural[:, :128], (((1,), (1,)), ((), ())), precision=HIGHEST,
        preferred_element_type=f32,
    )


def lanes_to_cells(rows):
    return lax.dot_general(
        rows, unit_rows(), (((0,), (0,)), ((), ())), precision=HIGHEST, preferred_element_type=f32
    )


def live_mass(mass, count):
    slot = lax.broadcasted_iota(i32, (CELLS, 256), 1)
    return jnp.where(slot < count, mass, 0.0)


def pack_kernel(pos, vel, mass, smooth, entropy, stored, count, flags, sent, table, faces):
    fields = [pos[c].reshape(CELLS, 256) for c in range(3)]
    fields.append(live_mass(mass[...].reshape(CELLS, 256), count[...]))
    fields.append(smooth[...].reshape(CELLS, 256))
    fields += [vel[c].reshape(CELLS, 256) for c in range(3)]
    fields += [entropy[...].reshape(CELLS, 256), stored[...].reshape(CELLS, 256)]
    for f, field in enumerate(fields):
        table[8 * f : 8 * f + 8, :] = cells_to_lanes(field)
    table[FLAGS:ROWS, :] = flags[...]
    faces[...] = picked(table[...], sent[0:1, :])


def segment_units():
    row = lax.broadcasted_iota(i32, (24, 256), 0) % 8
    lane = lax.broadcasted_iota(i32, (24, 256), 1)
    return (row == lane // 128 * 4 + lane % 128 // 32).astype(f32)


def store_rows(target, feature, rows):
    high = rows.astype(jnp.bfloat16).astype(f32)
    rest = rows - high
    middle = rest.astype(jnp.bfloat16).astype(f32)
    parts = jnp.concatenate([high, middle, rest - middle], 0)
    spread = lax.dot_general(
        parts, segment_units(), (((0,), (0,)), ((), ())), preferred_element_type=f32
    )
    for group in range(2):
        for block in range(LANES // 8):
            at = (group * LANES + block * 8) * HELD + feature
            target[pl.ds(at, 8, stride=HELD), :] = spread[
                8 * block : 8 * block + 8, 128 * group : 128 * group + 128
            ]


def store_columns(target, feature, block, count, natural):
    part = lax.broadcasted_iota(i32, (8, 128), 1) // 32
    for half in range(2):
        slots = natural[:, 128 * half : 128 * half + 128]
        turns = [slots] + [pltpu.roll(slots, 32 * t, 1) for t in range(1, 4)]
        for k in range(4):
            value = turns[(0 - k) % 4]
            for r in range(1, 4):
                value = jnp.where(part == r, turns[(r - k) % 4], value)
            at = (block * 8 * count + feature) * 8 + half * 4 + k
            target.reshape((CELLS + 1) * count * 8, 128)[pl.ds(at, 8, stride=count * 8), :] = value


def build_lists(table, coord, list_d, list_f, count_d, count_f):
    active = lax.broadcasted_iota(i32, (8, LANES), 0).astype(f32) < table[LIVE : LIVE + 1, :]
    reach = 4.0 * table[32:40, :] * table[32:40, :] * 1.0001
    squares = []
    for c in range(3):
        p = table[8 * c : 8 * c + 8, :]
        squares.append({-1: p * p, 0: None, 1: (1.0 - p) * (1.0 - p)})
    far = jnp.where(active, 0.0, 1e9)
    cx, cy, cz = coord[0:1, :], coord[1:2, :], coord[2:3, :]
    entries_d, entries_f = [], []
    kept_d = kept_f = jnp.zeros((2, LANES), i32)
    center = 13
    offsets = OFFSETS[:center] + [(0, 0, 0)] + OFFSETS[center:]
    for k, (ox, oy, oz) in enumerate(offsets):
        away = far
        for c, o in enumerate((ox, oy, oz)):
            if o:
                away = away + squares[c][o]
        bx, by, bz = cx + ox, cy + oy, cz + oz
        ok = (bx >= 0) & (bx < BX) & (by >= 0) & (by < BY) & (bz >= 0) & (bz < BZ)
        if k != center:
            row = FLAGS + (k if k < center else k - 1)
            ok = ok & (table[row : row + 1, :] > 0.5)
        cell = (bx * BY + by) * BZ + bz
        over_d = away - reach
        over_f = away - 1.0001

        def near(over):
            return jnp.concatenate(
                [jnp.min(over[0:4], 0, keepdims=True), jnp.min(over[4:8], 0, keepdims=True)], 0
            )

        both = jnp.concatenate([cell, cell], 0)
        oks = jnp.concatenate([ok.astype(i32), ok.astype(i32)], 0) > 0
        for over, entries, which in ((over_d, entries_d, 0), (over_f, entries_f, 1)):
            keep = oks & (near(over) <= 0.0)
            kept = kept_d if which == 0 else kept_f
            entries.append(jnp.where(keep, both + (k - kept) * 1024, NONE))
            if which == 0:
                kept_d = kept + keep.astype(i32)
            else:
                kept_f = kept + keep.astype(i32)
    for entries, target, kept, counted in (
        (entries_d, list_d, kept_d, count_d), (entries_f, list_f, kept_f, count_f),
    ):
        for bit in range(5):
            step, mask = 1 << bit, 1024 << bit
            moves = [(e & mask) != 0 for e in entries]
            moved = []
            for p in range(27):
                e = jnp.where(moves[p], NONE, entries[p])
                if p + step < 27:
                    e = jnp.where(moves[p + step], entries[p + step], e)
                moved.append(e)
            entries = moved
        entries = [e & 1023 for e in entries]
        for p in range(WORDS):
            word = entries[3 * p] + (entries[3 * p + 1] << 10) + (entries[3 * p + 2] << 20)
            for group in range(2):
                for t in range(TILES):
                    at = (p * 2 + group) * TILES + t
                    target[at : at + 1, :] = word[group : group + 1, 128 * t : 128 * t + 128]
        target[WORDS * 2 * TILES :, :] = jnp.full((LIST_ROWS - WORDS * 2 * TILES, 128), NONE, i32)
        for group in range(2):
            for t in range(TILES):
                counted[group * TILES + t : group * TILES + t + 1, :] = kept[
                    group : group + 1, 128 * t : 128 * t + 128
                ]
        counted[2 * TILES :, :] = jnp.zeros((16 - 2 * TILES, 128), i32)


def work_items(counts, items_v, items_s, ends, ends_v, ends_s, sem):
    items = jnp.floor((counts[...] + SPAN - 1).astype(f32) * (1.00002 / SPAN))
    row = lax.broadcasted_iota(i32, (128, 128), 0)
    lane = lax.broadcasted_iota(i32, (128, 128), 1)
    within = jnp.dot(items, (row <= lane).astype(f32), preferred_element_type=f32)
    whole = jnp.broadcast_to(within[:, 127:128], (16, 128))
    earlier = (
        lax.broadcasted_iota(i32, (16, 16), 1) < lax.broadcasted_iota(i32, (16, 16), 0)
    ).astype(f32)
    end = within + jnp.dot(earlier, whole, precision=HIGHEST, preferred_element_type=f32)
    ends_v[...] = end
    copy = pltpu.make_async_copy(ends_v, ends_s, sem)
    copy.start()
    for t in range(2 * TILES):
        ends[128 * t : 128 * t + 128, :] = jnp.broadcast_to(end[t : t + 1, :], (128, 128)).T
    items_v[...] = jnp.full((ITEM_ROWS, 128), (GROUPS - 1) * 2049, i32)
    copy.wait()
    last = [ends_s[t, 127].astype(i32) for t in range(2 * TILES)]
    total = last[-1]
    lanes = lax.broadcasted_iota(i32, (8, 128), 1)

    def fill(j, _):
        first = j * 128
        index = first + lanes
        number = index.astype(f32)
        begin = jnp.int32(0)
        stop = jnp.int32(0)
        before = jnp.int32(0)
        for e in last:
            begin = begin + (e <= first).astype(i32)
            stop = stop + (e <= first + 127).astype(i32)
            before = jnp.where(e <= first, e, before)
        stop = jnp.minimum(stop + 1, 2 * TILES)

        def tile(t, carry):
            passed, start = carry
            for u in range(16):
                e = ends[pl.ds(pl.multiple_of(t * 128 + u * 8, 8), 8), :]
                over = e <= number
                passed = passed + jnp.where(over, 1.0, 0.0)
                start = jnp.maximum(start, jnp.where(over, e, 0.0))
            return passed, start

        zero = jnp.zeros((8, 128), f32)
        passed, start = lax.fori_loop(begin, stop, tile, (zero, zero))
        group = begin * 128 + jnp.sum(passed, 0, keepdims=True).astype(i32)
        start = jnp.maximum(jnp.max(start, 0, keepdims=True).astype(i32), before)
        code = group + ((index[0:1] - start) * GROUPS + group) * 2048
        items_v[pl.ds(j, 1), :] = jnp.where(index[0:1] < total, code, (GROUPS - 1) * 2049)
        return 0

    lax.fori_loop(0, (total + 127) >> 7, fill, 0)
    copy = pltpu.make_async_copy(items_v, items_s, sem)
    copy.start()
    copy.wait()
    return total


def run_items(total, batch, items, lists, item, add):
    per_row = 128 // batch

    def take(turn):
        codes = [items[turn // per_row, (turn % per_row) * batch + u] for u in range(batch)]
        return codes, [lists[code >> 18, (code >> 11) & 127] for code in codes]

    def step(turn, carry):
        codes, words = carry
        later = take(turn + 1)
        results = []
        for code, word in zip(codes, words):
            group = code & 2047
            results.append((group, item(group, (word & 1023, (word >> 10) & 1023, word >> 20))))
        for group, values in results:
            add(group, values)
        return later

    lax.fori_loop(0, (total + batch - 1) // batch, step, take(jnp.int32(0)))


def row_sums(tiles, part_index, count, reduced):
    def block(i, _):
        for u in range(16):
            value = None
            for s in range(8):
                at = ((i * 128 + u * 8) * count + part_index) * 8 + s
                part = tiles.reshape(GROUPS * count * 8, 128)[pl.ds(at, 8, stride=8 * count), :]
                value = part if value is None else value + part
            reduced[pl.ds(pl.multiple_of(i * 128 + u * 8, 8), 8), :] = value
        return 0

    lax.fori_loop(0, GROUPS // 128, block, 0)
    row = lax.broadcasted_iota(i32, (8, 128), 0)
    segment = lax.broadcasted_iota(i32, (8, 128), 1) // 32
    out = None
    for group in range(2):
        values = reduced[LANES * group : LANES * group + LANES, :]
        unit = (row == segment + 4 * group).astype(f32)
        high = values.astype(jnp.bfloat16).astype(f32)
        for part in (high, values - high):
            term = lax.dot_general(
                unit, part, (((1,), (1,)), ((), ())), preferred_element_type=f32
            )
            out = term if out is None else out + term
    return out


def density_kernel(
    parts, coord, source, pos, mass, count, table, list_f, count_f, sums,
    list_v, count_v, list_s, items_v, items_s, ends, ends_v, ends_s, rows, columns, total, reduced,
    natural, sem,
):
    table[...] = picked(parts[...], source[0:1, :])
    build_lists(table, coord, list_v, list_f, count_v, count_f)
    list_copy = pltpu.make_async_copy(list_v, list_s, sem.at[0])
    list_copy.start()
    place = coord[...].astype(f32)
    for c in range(3):
        store_rows(rows, c, table[8 * c : 8 * c + 8, :] + place[c : c + 1, :])
    smooth = table[32:40, :]
    home = lax.broadcasted_iota(i32, (8, LANES), 1) < EXT
    safe = jnp.where(home, smooth, 1.0)
    store_rows(rows, 3, 1.0 / safe)
    for c in range(3):
        natural[c] = pos[c].reshape(CELLS, 256)
    natural[3] = live_mass(mass[...].reshape(CELLS, 256), count[...])

    def fill_block(block):
        start = pl.ds(pl.multiple_of(block * 8, 8), 8)
        cell = block * 8 + lax.broadcasted_iota(i32, (8, 256), 0)
        for c, value in enumerate((cell // 16, (cell // 4) % 4, cell % 4)):
            store_columns(columns, c, block, 4, natural[c, start, :] + value.astype(f32))
        store_columns(columns, 3, block, 4, natural[3, start, :])

    def fill(step, _):
        for u in range(4):
            fill_block(step * 4 + u)
        return 0

    lax.fori_loop(0, CELLS // 32, fill, 0)
    columns[NONE] = jnp.zeros((4, 8, 128), f32)
    total[...] = jnp.zeros_like(total)
    list_copy.wait()

    def item(group, cells):
        row = [rows[pl.ds(group * HELD + f, 8, stride=0), :] for f in range(4)]
        acc = None
        for cell in cells:
            col = [columns[cell, f] for f in range(4)]
            d = [row[c] - col[c] for c in range(3)]
            r2 = d[0] * d[0] + d[1] * d[1] + d[2] * d[2]
            r = r2 * lax.rsqrt(jnp.maximum(r2, 1e-30))
            u = jnp.maximum(2.0 - r * row[3], 0.0)
            v = jnp.maximum(u - 1.0, 0.0)
            term = col[3] * (u * u * u - 4.0 * (v * v * v))
            acc = term if acc is None else acc + term
        return acc

    def add(group, value):
        total[group, 0] = total[group, 0] + value

    number = work_items(count_v, items_v, items_s, ends, ends_v, ends_s, sem.at[1])
    run_items(number, BATCH_D, items_s, list_s, item, add)
    scale = 1.0 / (4.0 * math.pi * safe * safe * safe)
    sums[...] = row_sums(total, 0, 1, reduced) * scale


def joined(sums, along_y, along_z, along_both, coord, shared):
    def matched(values, axis):
        step, extent = ((EZ, BY), (1, BZ))[axis - 1]
        position = coord[axis : axis + 1, :]
        low = position == 0
        high = position == extent - 1
        if shared:
            low = low | (position == -1)
            high = high | (position == extent)
        by = extent * step
        ahead = pltpu.roll(values, LANES - by, 1)
        behind = pltpu.roll(values, by, 1)
        return jnp.where(low, ahead, jnp.where(high, behind, 0.0))

    return (
        sums[...] + matched(along_y[...], 1) + matched(along_z[...], 2)
        + matched(matched(along_both[...], 1), 2)
    )


def home_lanes():
    cell = np.arange(CELLS)
    lane = ((cell // 16 + 1) * EY + (cell // 4) % 4 + 1) * EZ + cell % 4 + 1
    return np.tile(lane.astype(np.int32), (8, 1))


def state(entropy, density):
    pressure = entropy * jnp.exp(jnp.log(density) * (-1.0 / 3.0))
    return pressure, jnp.sqrt(ADIABATIC * pressure * density)


def force_kernel(
    table, fresh, fresh_y, fresh_z, fresh_yz, list_v, count_v, coord, home, pos, vel, mass, smooth, entropy, stored, count,
    active, sums, density, list_s, items_v, items_s, ends, ends_v, ends_s, rows, columns, total, reduced,
    natural, sem,
):
    list_copy = pltpu.make_async_copy(list_v, list_s, sem.at[0])
    list_copy.start()
    is_cell = lax.broadcasted_iota(i32, (8, LANES), 1) < EXT
    live = lax.broadcasted_iota(i32, (8, LANES), 0).astype(f32) < table[LIVE : LIVE + 1, :]
    place = coord[...].astype(f32)

    def field(f):
        return table[8 * f : 8 * f + 8, :]

    now = joined(fresh, fresh_y, fresh_z, fresh_yz, coord, True)
    rho = jnp.where(is_cell, jnp.where(live, now, field(9)), 1.0)
    row_h = jnp.where(is_cell, field(4), 1.0)
    row_p, row_s = state(field(8), rho)

    def features(h, sound, dens, pressure):
        a = math.sqrt(0.75 / math.pi) / (h * h)
        return 2.0 * a, a / h, 0.05 * h, 0.5 * sound, 2.0 * dens, pressure

    for c in range(3):
        store_rows(rows, c, field(c) + place[c : c + 1, :])
        store_rows(rows, 3 + c, 20.0 * field(5 + c))
    for f, value in enumerate(features(row_h, row_s, rho, row_p)):
        store_rows(rows, 6 + f, value)

    slot = lax.broadcasted_iota(i32, (CELLS, 128), 1)
    updated = lanes_to_cells(picked(rho, home[0:1, :]))
    old = stored[...].reshape(CELLS, 256)
    new = jnp.concatenate([jnp.where(slot < active[...], updated, old[:, :128]), old[:, 128:]], 1)
    density[...] = new.reshape(BX, BY, BZ, 256)
    for c in range(3):
        natural[c] = pos[c].reshape(CELLS, 256)
        natural[3 + c] = vel[c].reshape(CELLS, 256)
    natural[6] = live_mass(mass[...].reshape(CELLS, 256), count[...])
    natural[7] = smooth[...].reshape(CELLS, 256)
    natural[8] = entropy[...].reshape(CELLS, 256)
    natural[9] = new

    def fill_block(block):
        start = pl.ds(pl.multiple_of(block * 8, 8), 8)
        cell = block * 8 + lax.broadcasted_iota(i32, (8, 256), 0)
        for c, value in enumerate((cell // 16, (cell // 4) % 4, cell % 4)):
            store_columns(columns, c, block, 13, natural[c, start, :] + value.astype(f32))
            store_columns(columns, 3 + c, block, 13, 20.0 * natural[3 + c, start, :])
        dens = natural[9, start, :]
        pressure, sound = state(natural[8, start, :], dens)
        for f, value in enumerate(features(natural[7, start, :], sound, dens, pressure)):
            store_columns(columns, 6 + f, block, 13, value)
        store_columns(columns, 12, block, 13, natural[6, start, :])

    def fill(step, _):
        for u in range(2):
            fill_block(step * 2 + u)
        return 0

    lax.fori_loop(0, CELLS // 16, fill, 0)
    columns[NONE] = jnp.ones((13, 8, 128), f32)
    columns[NONE, 12] = jnp.zeros((8, 128), f32)
    total[...] = jnp.zeros_like(total)
    list_copy.wait()

    def item(group, cells):
        row = [rows[pl.ds(group * HELD + f, 8, stride=0), :] for f in range(12)]
        acc = [None] * 3
        for cell in cells:
            col = [columns[cell, f] for f in range(13)]
            d = [row[c] - col[c] for c in range(3)]
            r2 = d[0] * d[0] + d[1] * d[1] + d[2] * d[2]
            closing = (
                (row[3] - col[3]) * d[0] + (row[4] - col[4]) * d[1] + (row[5] - col[5]) * d[2]
            )
            inverse = lax.rsqrt(jnp.maximum(r2, 1e-30))
            r = r2 * inverse

            def slope(twice, per):
                t = per * r
                u = jnp.maximum(twice - t, 0.0)
                s = jnp.minimum(t, u)
                return s * (u + (u - s))

            h = row[8] + col[8]
            approach = (h * jnp.minimum(closing, 0.0)) * pl.reciprocal(r2 + h * h, approx=True)
            viscosity = (approach * (approach - (row[9] + col[9]))) * pl.reciprocal(
                row[10] + col[10], approx=True
            )
            weight = (row[11] + viscosity) * slope(row[6], row[7])
            weight = weight + (col[11] + viscosity) * slope(col[6], col[7])
            weight = weight * (inverse * col[12])
            for c in range(3):
                term = weight * d[c]
                acc[c] = term if acc[c] is None else acc[c] + term
        return acc

    def add(group, values):
        for c in range(3):
            total[group, c] = total[group, c] + values[c]

    number = work_items(count_v, items_v, items_s, ends, ends_v, ends_s, sem.at[1])
    run_items(number, BATCH_F, items_s, list_s, item, add)
    for c in range(3):
        sums[8 * c : 8 * c + 8, :] = row_sums(total, c, 3, reduced)


def spread_kernel(pushed, pushed_y, pushed_z, pushed_yz, coord, home, active, out):
    whole = joined(pushed, pushed_y, pushed_z, pushed_yz, coord, False)
    mine = picked(whole, home[0:1, :])
    slot = lax.broadcasted_iota(i32, (CELLS, 128), 1)
    for c in range(3):
        rows = lanes_to_cells(mine[8 * c : 8 * c + 8, :])
        rows = jnp.where(slot < active[...], rows, 0.0)
        out[c] = jnp.concatenate([rows, jnp.zeros((CELLS, 128), f32)], 1).reshape(BX, BY, BZ, 256)


VMEM_SPEC = pl.BlockSpec(memory_space=pltpu.VMEM)
SMEM_SPEC = pl.BlockSpec(memory_space=pltpu.SMEM)
PARAMS = pltpu.CompilerParams(vmem_limit_bytes=56 * 1024 * 1024)


def shape(*dims, dtype=f32):
    return jax.ShapeDtypeStruct(dims, dtype)


def call(kernel, inputs, outputs, in_specs=None, scratch=()):
    single = not isinstance(outputs, (list, tuple))
    return pl.pallas_call(
        kernel,
        out_shape=outputs,
        in_specs=in_specs or [VMEM_SPEC] * len(inputs),
        out_specs=VMEM_SPEC if single else [VMEM_SPEC] * len(outputs),
        scratch_shapes=list(scratch),
        compiler_params=PARAMS,
    )(*inputs)


def item_scratch():
    return [
        pltpu.VMEM((ITEM_ROWS, 128), i32), pltpu.SMEM((ITEM_ROWS, 128), i32),
        pltpu.VMEM((GROUPS, 128), f32), pltpu.VMEM((16, 128), f32), pltpu.SMEM((16, 128), f32),
    ]


def density_scratch():
    return [
        pltpu.VMEM((LIST_ROWS, 128), i32), pltpu.VMEM((16, 128), i32), pltpu.SMEM((LIST_ROWS, 128), i32),
        *item_scratch(), pltpu.VMEM((GROUPS * HELD, 128), f32), pltpu.VMEM((CELLS + 1, 4, 8, 128), f32),
        pltpu.VMEM((GROUPS, 1, 8, 128), f32), pltpu.VMEM((GROUPS, 128), f32),
        pltpu.VMEM((4, CELLS, 256), f32), pltpu.SemaphoreType.DMA((2,)),
    ]


def force_scratch():
    return [
        pltpu.SMEM((LIST_ROWS, 128), i32), *item_scratch(), pltpu.VMEM((GROUPS * HELD, 128), f32), pltpu.VMEM((CELLS + 1, 13, 8, 128), f32),
        pltpu.VMEM((GROUPS, 3, 8, 128), f32), pltpu.VMEM((GROUPS, 128), f32),
        pltpu.VMEM((10, CELLS, 256), f32), pltpu.SemaphoreType.DMA((2,)),
    ]


def ring(axis, by):
    devices = lax.axis_size(axis)
    return [(i, (i + by) % devices) for i in range(devices)]


def first_exchange(table, faces):
    y_part, z_part, edge = faces[:, :128], faces[:, 128:256], faces[:, 256:320]
    y_in, z_in, edge_in = (
        lax.ppermute(part, ("gy", "gz"), pairs)
        for part, pairs in zip((y_part, z_part, edge), ACROSS)
    )
    low = jnp.concatenate([table[:, :16], y_in[:, :8], z_in[:, :8], edge_in[:, :4]], 1)
    high = jnp.concatenate([table[:, 240:], y_in[:, 120:], z_in[:, 120:], edge_in[:, 60:]], 1)
    before = lax.ppermute(high, "gx", ring("gx", 1))
    after = lax.ppermute(low, "gx", ring("gx", -1))
    unused = jnp.zeros((ROWS, LANES - EXT), f32)
    return jnp.concatenate([table, y_in, z_in, edge_in, before, after, unused], 1)


ACROSS = (
    [(0, 2), (1, 3), (2, 0), (3, 1)],
    [(0, 1), (1, 0), (2, 3), (3, 2)],
    [(0, 3), (1, 2), (2, 1), (3, 0)],
)


def sent_across(sums):
    return [lax.ppermute(sums, ("gy", "gz"), pairs) for pairs in ACROSS]


def shared_sums(sums):
    plane = EY * EZ
    top = BX * plane
    before = lax.ppermute(sums[:, top : top + 2 * plane], "gx", ring("gx", 1))
    after = lax.ppermute(sums[:, : 2 * plane], "gx", ring("gx", -1))
    middle = sums[:, 2 * plane : top]
    return jnp.concatenate(
        [sums[:, : 2 * plane] + before, middle, sums[:, top:EXT] + after, sums[:, EXT:]], 1
    )


def returned_sums(sums):
    plane = EY * EZ
    top = BX * plane
    before = lax.ppermute(sums[:, top + plane : EXT], "gx", ring("gx", 1))
    after = lax.ppermute(sums[:, :plane], "gx", ring("gx", -1))
    return jnp.concatenate(
        [
            sums[:, :plane],
            sums[:, plane : 2 * plane] + before,
            sums[:, 2 * plane : top],
            sums[:, top : top + plane] + after,
            sums[:, top + plane :],
        ],
        1,
    )


def shards(pos, vel, mass, smooth, entropy, stored, particle_count, active_count, pair_side):
    coord_np, source_np = maps()
    coord, source = jnp.asarray(coord_np), jnp.asarray(source_np)
    home = jnp.asarray(home_lanes())
    count = particle_count.reshape(CELLS, 1)
    active = active_count.reshape(CELLS, 1)
    flags = jnp.concatenate(
        [
            pair_side.reshape(26, CELLS).astype(f32),
            active_count.reshape(1, CELLS).astype(f32),
            jnp.zeros((ROWS - FLAGS - 27, CELLS), f32),
        ],
        0,
    )
    inputs = (pos, vel, mass, smooth, entropy, stored, count, flags, jnp.asarray(sent_cells()))
    table, faces = call(pack_kernel, inputs, [shape(ROWS, CELLS), shape(ROWS, 384)])
    parts = first_exchange(table, faces)
    inputs = (parts, coord, source, pos, mass, count)
    table, list_f, count_f, sums = call(
        density_kernel,
        inputs,
        [
            shape(ROWS, LANES), shape(LIST_ROWS, 128, dtype=i32), shape(16, 128, dtype=i32),
            shape(ACT, LANES),
        ],
        scratch=density_scratch(),
    )
    fresh = shared_sums(sums)
    inputs = (
        table, fresh, *sent_across(fresh), list_f, count_f, coord, home, pos, vel, mass, smooth, entropy, stored,
        count, active,
    )
    sums, density = call(
        force_kernel,
        inputs,
        [shape(24, LANES), shape(BX, BY, BZ, 256)],

        scratch=force_scratch(),
    )
    pushed = returned_sums(sums)
    inputs = (pushed, *sent_across(pushed), coord, home, active)
    acceleration = call(spread_kernel, inputs, shape(3, BX, BY, BZ, 256))
    return density, acceleration


def solution(mesh):
    cells = P("gx", "gy", "gz", None)
    vectors = P(None, "gx", "gy", "gz", None)
    counts = P("gx", "gy", "gz")
    in_specs = (
        vectors, vectors, cells, cells, cells, cells, counts, counts, P(None, "gx", "gy", "gz"),
    )
    return jax.shard_map(
        shards, mesh=mesh, in_specs=in_specs, out_specs=(cells, vectors), check_vma=False
    )
```

```python
import functools
import math

import jax
import jax.numpy as jnp
import numpy as np
from jax import lax
from jax.experimental import pallas as pl
from jax.experimental.pallas import tpu as pltpu
from jax.sharding import PartitionSpec as P

ACT = 8
BX, BY, BZ = 16, 4, 4
CELLS = BX * BY * BZ
EX, EY, EZ = BX + 2, BY + 2, BZ + 2
EXT = EX * EY * EZ
LANES = 768
TILES = LANES // 128
GROUPS = 2 * LANES
ROWS = 112
FLAGS = 80
LIVE = 106
SPAN = 3
WORDS = 9
ITEM_ROWS = 96
LIST_ROWS = 112
HELD = 13
BATCH_D = 8
BATCH_F = 8
NONE = CELLS
ADIABATIC = 5.0 / 3.0
HIGHEST = lax.Precision.HIGHEST
f32 = jnp.float32
i32 = jnp.int32

OFFSETS = [
    (a, b, c) for a in (-1, 0, 1) for b in (-1, 0, 1) for c in (-1, 0, 1) if (a, b, c) != (0, 0, 0)
]


def maps():
    coord = np.full((8, LANES), -9, np.int32)
    coord[:3] = -5
    source = np.full((8, LANES), -1, np.int32)
    for x in range(-1, BX + 1):
        for y in range(-1, BY + 1):
            for z in range(-1, BZ + 1):
                lane = ((x + 1) * EY + y + 1) * EZ + z + 1
                coord[0, lane], coord[1, lane], coord[2, lane] = x, y, z
                inside_y, inside_z = 0 <= y < BY, 0 <= z < BZ
                face_y = 0 if y == BY else 1
                face_z = 0 if z == BZ else 1
                def place(width_home, width_y, width_z, width_yz, starts, row):
                    if inside_y and inside_z:
                        return starts[0] + row * width_home + y * BZ + z
                    if inside_z:
                        return starts[1] + row * width_y + face_y * BZ + z
                    if inside_y:
                        return starts[2] + row * width_z + y * 2 + face_z
                    return starts[3] + row * width_yz + face_y * 2 + face_z

                if 0 <= x < BX:
                    at = place(16, 8, 8, 4, (0, 256, 384, 512), x)
                else:
                    base = 576 if x < 0 else 612
                    at = place(16, 8, 8, 4, (base, base + 16, base + 24, base + 32), 0)
                source[0, lane] = at
    return coord, source


def sent_cells():
    table = np.full((8, 384), -1, np.int32)
    for x in range(BX):
        for face in range(2):
            for z in range(BZ):
                table[0, x * 8 + face * BZ + z] = (x * BY + (0 if face == 0 else BY - 1)) * BZ + z
            for y in range(BY):
                table[0, 128 + x * 8 + y * 2 + face] = (x * BY + y) * BZ + (
                    0 if face == 0 else BZ - 1
                )
            for other in range(2):
                table[0, 256 + x * 4 + face * 2 + other] = (
                    x * BY + (0 if face == 0 else BY - 1)
                ) * BZ + (0 if other == 0 else BZ - 1)
    return table


def picked(values, source_row):
    count, size = values.shape
    rows = lax.broadcasted_iota(i32, (size, source_row.shape[1]), 0)
    chosen = (rows == source_row).astype(f32).astype(jnp.bfloat16)
    high = values.astype(jnp.bfloat16).astype(f32)
    rest = values - high
    middle = rest.astype(jnp.bfloat16).astype(f32)
    parts = jnp.concatenate([high, middle, rest - middle], 0).astype(jnp.bfloat16)
    out = jnp.dot(parts, chosen, preferred_element_type=f32)
    return out[:count] + out[count : 2 * count] + out[2 * count :]


def unit_rows():
    return (
        lax.broadcasted_iota(i32, (ACT, 128), 0) == lax.broadcasted_iota(i32, (ACT, 128), 1)
    ).astype(f32)


def cells_to_lanes(natural):
    return lax.dot_general(
        unit_rows(), natural[:, :128], (((1,), (1,)), ((), ())), precision=HIGHEST,
        preferred_element_type=f32,
    )


def lanes_to_cells(rows):
    return lax.dot_general(
        rows, unit_rows(), (((0,), (0,)), ((), ())), precision=HIGHEST, preferred_element_type=f32
    )


def live_mass(mass, count):
    slot = lax.broadcasted_iota(i32, (CELLS, 256), 1)
    return jnp.where(slot < count, mass, 0.0)


def pack_kernel(pos, vel, mass, smooth, entropy, stored, count, flags, sent, table, y_part, z_part, edge, low, high):
    fields = [pos[c].reshape(CELLS, 256) for c in range(3)]
    fields.append(live_mass(mass[...].reshape(CELLS, 256), count[...]))
    fields.append(smooth[...].reshape(CELLS, 256))
    fields += [vel[c].reshape(CELLS, 256) for c in range(3)]
    fields += [entropy[...].reshape(CELLS, 256), stored[...].reshape(CELLS, 256)]
    for f, field in enumerate(fields):
        table[8 * f : 8 * f + 8, :] = cells_to_lanes(field)
    table[FLAGS:ROWS, :] = flags[...]
    faces = picked(table[...], sent[0:1, :])
    y_part[...] = faces[:, :128]
    z_part[...] = faces[:, 128:256]
    edge[...] = faces[:, 256:320]
    low[...] = table[:, :16]
    high[...] = table[:, CELLS - 16 :]


def segment_units():
    row = lax.broadcasted_iota(i32, (24, 256), 0) % 8
    lane = lax.broadcasted_iota(i32, (24, 256), 1)
    return (row == lane // 128 * 4 + lane % 128 // 32).astype(f32)


def store_rows(target, feature, rows):
    high = rows.astype(jnp.bfloat16).astype(f32)
    rest = rows - high
    middle = rest.astype(jnp.bfloat16).astype(f32)
    parts = jnp.concatenate([high, middle, rest - middle], 0)
    spread = lax.dot_general(
        parts, segment_units(), (((0,), (0,)), ((), ())), preferred_element_type=f32
    )
    for group in range(2):
        for block in range(LANES // 8):
            at = (group * LANES + block * 8) * HELD + feature
            target[pl.ds(at, 8, stride=HELD), :] = spread[
                8 * block : 8 * block + 8, 128 * group : 128 * group + 128
            ]


def store_columns(target, feature, block, count, natural):
    part = lax.broadcasted_iota(i32, (8, 128), 1) // 32
    for half in range(2):
        slots = natural[:, 128 * half : 128 * half + 128]
        turns = [slots] + [pltpu.roll(slots, 32 * t, 1) for t in range(1, 4)]
        for k in range(4):
            value = turns[(0 - k) % 4]
            for r in range(1, 4):
                value = jnp.where(part == r, turns[(r - k) % 4], value)
            at = (block * 8 * count + feature) * 8 + half * 4 + k
            target.reshape((CELLS + 1) * count * 8, 128)[pl.ds(at, 8, stride=count * 8), :] = value


def build_lists(table, coord, list_d, list_f, count_d, count_f):
    row = lax.broadcasted_iota(i32, (8, LANES), 0)
    active = row.astype(f32) < table[LIVE : LIVE + 1, :]
    reach = 4.0 * table[32:40, :] * table[32:40, :] * 1.0001
    for_density = row % 4 == 3
    far = jnp.where(active, 0.0, 1e9)
    squares, inside, cells = [], [], []
    for c, (extent, step) in enumerate(((BX, BY * BZ), (BY, BZ), (BZ, 1))):
        p = table[8 * c : 8 * c + 8, :]
        squares.append({-1: p * p, 1: (1.0 - p) * (1.0 - p)})
        at = jnp.broadcast_to(coord[c : c + 1, :], (8, LANES))
        inside.append({o: (at + o >= 0) & (at + o < extent) for o in (-1, 0, 1)})
        cells.append(at * step)
    base = cells[0] + cells[1] + cells[2]

    def nearest(values):
        values = jnp.minimum(values, pltpu.roll(values, 1, 0))
        return jnp.minimum(values, pltpu.roll(values, 2, 0))

    entries = []
    kept = jnp.zeros((8, LANES), i32)
    center = 13
    offsets = OFFSETS[:center] + [(0, 0, 0)] + OFFSETS[center:]
    for k, (ox, oy, oz) in enumerate(offsets):
        away = far
        for c, o in enumerate((ox, oy, oz)):
            if o:
                away = away + squares[c][o]
        keep = inside[0][ox] & inside[1][oy] & inside[2][oz]
        if k != center:
            flag = FLAGS + (k if k < center else k - 1)
            keep = keep & (table[flag : flag + 1, :] > 0.5)
        over = jnp.where(
            for_density, nearest(away - reach), pltpu.roll(nearest(away - 1.0001), 7, 0)
        )
        keep = keep & (over <= 0.0)
        cell = base + ((ox * BY + oy) * BZ + oz + k * 1024)
        entries.append(jnp.where(keep, cell - kept * 1024, NONE))
        kept = kept + keep.astype(i32)
    for bit in range(5):
        step, mask = 1 << bit, 1024 << bit
        moves = [(e & mask) != 0 for e in entries]
        moved = []
        for p in range(27):
            e = jnp.where(moves[p], NONE, entries[p])
            if p + step < 27:
                e = jnp.where(moves[p + step], entries[p + step], e)
            moved.append(e)
        entries = moved
    entries = [e & 1023 for e in entries]
    for p in range(WORDS):
        word = entries[3 * p] + (entries[3 * p + 1] << 10) + (entries[3 * p + 2] << 20)
        for group in range(2):
            for t in range(TILES):
                at = (p * 2 + group) * TILES + t
                for first, target in ((3, list_d), (2, list_f)):
                    target[at : at + 1, :] = word[
                        first + 4 * group : first + 4 * group + 1, 128 * t : 128 * t + 128
                    ]
    for first, target, counted in ((3, list_d, count_d), (2, list_f, count_f)):
        target[WORDS * 2 * TILES :, :] = jnp.full((LIST_ROWS - WORDS * 2 * TILES, 128), NONE, i32)
        for group in range(2):
            for t in range(TILES):
                counted[group * TILES + t : group * TILES + t + 1, :] = kept[
                    first + 4 * group : first + 4 * group + 1, 128 * t : 128 * t + 128
                ]
        counted[2 * TILES :, :] = jnp.zeros((16 - 2 * TILES, 128), i32)


def work_items(counts, items_v, items_s, ends, ends_v, ends_s, sem):
    items = jnp.floor((counts[...] + SPAN - 1).astype(f32) * (1.00002 / SPAN))
    row = lax.broadcasted_iota(i32, (128, 128), 0)
    lane = lax.broadcasted_iota(i32, (128, 128), 1)
    within = jnp.dot(items, (row <= lane).astype(f32), preferred_element_type=f32)
    whole = jnp.broadcast_to(within[:, 127:128], (16, 128))
    earlier = (
        lax.broadcasted_iota(i32, (16, 16), 1) < lax.broadcasted_iota(i32, (16, 16), 0)
    ).astype(f32)
    end = within + jnp.dot(earlier, whole, precision=HIGHEST, preferred_element_type=f32)
    ends_v[...] = end
    copy = pltpu.make_async_copy(ends_v, ends_s, sem)
    copy.start()
    for t in range(2 * TILES):
        ends[128 * t : 128 * t + 128, :] = jnp.broadcast_to(end[t : t + 1, :], (128, 128)).T
    items_v[...] = jnp.full((ITEM_ROWS, 128), (GROUPS - 1) * 2049, i32)
    copy.wait()
    last = [ends_s[t, 127].astype(i32) for t in range(2 * TILES)]
    total = last[-1]
    lanes = lax.broadcasted_iota(i32, (8, 128), 1)

    def fill(j, _):
        first = j * 128
        index = first + lanes
        number = index.astype(f32)
        begin = jnp.int32(0)
        stop = jnp.int32(0)
        before = jnp.int32(0)
        for e in last:
            begin = begin + (e <= first).astype(i32)
            stop = stop + (e <= first + 127).astype(i32)
            before = jnp.where(e <= first, e, before)
        stop = jnp.minimum(stop + 1, 2 * TILES)

        def tile(t, carry):
            passed, start = carry
            for u in range(16):
                e = ends[pl.ds(pl.multiple_of(t * 128 + u * 8, 8), 8), :]
                over = e <= number
                passed = passed + jnp.where(over, 1.0, 0.0)
                start = jnp.maximum(start, jnp.where(over, e, 0.0))
            return passed, start

        zero = jnp.zeros((8, 128), f32)
        passed, start = lax.fori_loop(begin, stop, tile, (zero, zero))
        group = begin * 128 + jnp.sum(passed, 0, keepdims=True).astype(i32)
        start = jnp.maximum(jnp.max(start, 0, keepdims=True).astype(i32), before)
        code = group + ((index[0:1] - start) * GROUPS + group) * 2048
        items_v[pl.ds(j, 1), :] = jnp.where(index[0:1] < total, code, (GROUPS - 1) * 2049)
        return 0

    lax.fori_loop(0, (total + 127) >> 7, fill, 0)
    copy = pltpu.make_async_copy(items_v, items_s, sem)
    copy.start()
    copy.wait()
    return total


def run_items(total, batch, items, lists, item, add):
    per_row = 128 // batch
    bits = per_row.bit_length() - 1

    def take(turn):
        row, start = turn >> bits, (turn & (per_row - 1)) * batch
        codes = [items[row, start + u] for u in range(batch)]
        return codes, [lists[code >> 18, (code >> 11) & 127] for code in codes]

    def step(turn, carry):
        codes, words = carry
        results = []
        for code, word in zip(codes, words):
            group = code & 2047
            results.append((group, item(group, (word & 1023, (word >> 10) & 1023, word >> 20))))
        for group, values in results:
            add(group, values)
        return take(turn + 1)

    lax.fori_loop(0, (total + batch - 1) // batch, step, take(jnp.int32(0)))


def row_sums(tiles, part_index, count, reduced):
    def block(i, _):
        for u in range(16):
            value = None
            for s in range(8):
                at = ((i * 128 + u * 8) * count + part_index) * 8 + s
                part = tiles.reshape(GROUPS * count * 8, 128)[pl.ds(at, 8, stride=8 * count), :]
                value = part if value is None else value + part
            reduced[pl.ds(pl.multiple_of(i * 128 + u * 8, 8), 8), :] = value
        return 0

    lax.fori_loop(0, GROUPS // 128, block, 0)
    row = lax.broadcasted_iota(i32, (8, 128), 0)
    segment = lax.broadcasted_iota(i32, (8, 128), 1) // 32
    out = None
    for group in range(2):
        values = reduced[LANES * group : LANES * group + LANES, :]
        unit = (row == segment + 4 * group).astype(f32)
        high = values.astype(jnp.bfloat16).astype(f32)
        for part in (high, values - high):
            term = lax.dot_general(
                unit, part, (((1,), (1,)), ((), ())), preferred_element_type=f32
            )
            out = term if out is None else out + term
    return out


def density_kernel(
    parts, coord, source, pos, mass, count, table, list_f, count_f, sums,
    list_v, count_v, list_s, items_v, items_s, ends, ends_v, ends_s, rows, columns, total, reduced,
    natural, sem,
):
    table[...] = picked(parts[...], source[0:1, :])
    build_lists(table, coord, list_v, list_f, count_v, count_f)
    list_copy = pltpu.make_async_copy(list_v, list_s, sem.at[0])
    list_copy.start()
    place = coord[...].astype(f32)
    for c in range(3):
        store_rows(rows, c, table[8 * c : 8 * c + 8, :] + place[c : c + 1, :])
    smooth = table[32:40, :]
    home = lax.broadcasted_iota(i32, (8, LANES), 1) < EXT
    safe = jnp.where(home, smooth, 1.0)
    store_rows(rows, 3, 1.0 / safe)
    for c in range(3):
        natural[c] = pos[c].reshape(CELLS, 256)
    natural[3] = live_mass(mass[...].reshape(CELLS, 256), count[...])

    def fill_block(block):
        start = pl.ds(pl.multiple_of(block * 8, 8), 8)
        cell = block * 8 + lax.broadcasted_iota(i32, (8, 256), 0)
        for c, value in enumerate((cell // 16, (cell // 4) % 4, cell % 4)):
            store_columns(columns, c, block, 4, natural[c, start, :] + value.astype(f32))
        store_columns(columns, 3, block, 4, natural[3, start, :])

    def fill(step, _):
        for u in range(4):
            fill_block(step * 4 + u)
        return 0

    lax.fori_loop(0, CELLS // 32, fill, 0)
    columns[NONE] = jnp.zeros((4, 8, 128), f32)
    total[...] = jnp.zeros_like(total)
    list_copy.wait()

    def item(group, cells):
        row = [rows[pl.ds(group * HELD + f, 8, stride=0), :] for f in range(4)]
        acc = None
        for cell in cells:
            col = [columns[cell, f] for f in range(4)]
            d = [row[c] - col[c] for c in range(3)]
            r2 = d[0] * d[0] + d[1] * d[1] + d[2] * d[2]
            r = r2 * lax.rsqrt(jnp.maximum(r2, 1e-30))
            u = jnp.maximum(2.0 - r * row[3], 0.0)
            v = jnp.maximum(u - 1.0, 0.0)
            term = col[3] * (u * u * u - 4.0 * (v * v * v))
            acc = term if acc is None else acc + term
        return acc

    def add(group, value):
        total[group, 0] = total[group, 0] + value

    number = work_items(count_v, items_v, items_s, ends, ends_v, ends_s, sem.at[1])
    run_items(number, BATCH_D, items_s, list_s, item, add)
    scale = 1.0 / (4.0 * math.pi * safe * safe * safe)
    sums[...] = row_sums(total, 0, 1, reduced) * scale


def joined(sums, along_y, along_z, along_both, coord, shared):
    def matched(values, axis):
        step, extent = ((EZ, BY), (1, BZ))[axis - 1]
        position = coord[axis : axis + 1, :]
        low = position == 0
        high = position == extent - 1
        if shared:
            low = low | (position == -1)
            high = high | (position == extent)
        by = extent * step
        ahead = pltpu.roll(values, LANES - by, 1)
        behind = pltpu.roll(values, by, 1)
        return jnp.where(low, ahead, jnp.where(high, behind, 0.0))

    return (
        sums[...] + matched(along_y[...], 1) + matched(along_z[...], 2)
        + matched(matched(along_both[...], 1), 2)
    )


def home_lanes():
    cell = np.arange(CELLS)
    lane = ((cell // 16 + 1) * EY + (cell // 4) % 4 + 1) * EZ + cell % 4 + 1
    return np.tile(lane.astype(np.int32), (8, 1))


def state(entropy, density):
    pressure = entropy * jnp.exp(jnp.log(density) * (-1.0 / 3.0))
    return pressure, jnp.sqrt(ADIABATIC * pressure * density)


def force_kernel(
    table, fresh, fresh_y, fresh_z, fresh_yz, list_v, count_v, coord, home, pos, vel, mass, smooth, entropy, stored, count,
    active, sums, density, list_s, items_v, items_s, ends, ends_v, ends_s, rows, columns, total, reduced,
    natural, sem,
):
    list_copy = pltpu.make_async_copy(list_v, list_s, sem.at[0])
    list_copy.start()
    is_cell = lax.broadcasted_iota(i32, (8, LANES), 1) < EXT
    live = lax.broadcasted_iota(i32, (8, LANES), 0).astype(f32) < table[LIVE : LIVE + 1, :]
    place = coord[...].astype(f32)

    def field(f):
        return table[8 * f : 8 * f + 8, :]

    now = joined(fresh, fresh_y, fresh_z, fresh_yz, coord, True)
    rho = jnp.where(is_cell, jnp.where(live, now, field(9)), 1.0)
    row_h = jnp.where(is_cell, field(4), 1.0)
    row_p, row_s = state(field(8), rho)

    def features(h, sound, dens, pressure):
        a = math.sqrt(0.75 / math.pi) / (h * h)
        return 2.0 * a, a / h, 0.05 * h, 0.5 * sound, 2.0 * dens, pressure

    for c in range(3):
        store_rows(rows, c, field(c) + place[c : c + 1, :])
        store_rows(rows, 3 + c, 20.0 * field(5 + c))
    for f, value in enumerate(features(row_h, row_s, rho, row_p)):
        store_rows(rows, 6 + f, value)

    slot = lax.broadcasted_iota(i32, (CELLS, 128), 1)
    updated = lanes_to_cells(picked(rho, home[0:1, :]))
    old = stored[...].reshape(CELLS, 256)
    new = jnp.concatenate([jnp.where(slot < active[...], updated, old[:, :128]), old[:, 128:]], 1)
    density[...] = new.reshape(BX, BY, BZ, 256)
    for c in range(3):
        natural[c] = pos[c].reshape(CELLS, 256)
        natural[3 + c] = vel[c].reshape(CELLS, 256)
    natural[6] = live_mass(mass[...].reshape(CELLS, 256), count[...])
    natural[7] = smooth[...].reshape(CELLS, 256)
    natural[8] = entropy[...].reshape(CELLS, 256)
    natural[9] = new

    def fill_block(block):
        start = pl.ds(pl.multiple_of(block * 8, 8), 8)
        cell = block * 8 + lax.broadcasted_iota(i32, (8, 256), 0)
        for c, value in enumerate((cell // 16, (cell // 4) % 4, cell % 4)):
            store_columns(columns, c, block, 13, natural[c, start, :] + value.astype(f32))
            store_columns(columns, 3 + c, block, 13, 20.0 * natural[3 + c, start, :])
        dens = natural[9, start, :]
        pressure, sound = state(natural[8, start, :], dens)
        for f, value in enumerate(features(natural[7, start, :], sound, dens, pressure)):
            store_columns(columns, 6 + f, block, 13, value)
        store_columns(columns, 12, block, 13, natural[6, start, :])

    def fill(step, _):
        for u in range(2):
            fill_block(step * 2 + u)
        return 0

    lax.fori_loop(0, CELLS // 16, fill, 0)
    columns[NONE] = jnp.ones((13, 8, 128), f32)
    columns[NONE, 12] = jnp.zeros((8, 128), f32)
    total[...] = jnp.zeros_like(total)
    list_copy.wait()

    def item(group, cells):
        row = [rows[pl.ds(group * HELD + f, 8, stride=0), :] for f in range(12)]
        acc = [None] * 3
        for cell in cells:
            col = [columns[cell, f] for f in range(13)]
            d = [row[c] - col[c] for c in range(3)]
            r2 = d[0] * d[0] + d[1] * d[1] + d[2] * d[2]
            closing = (
                (row[3] - col[3]) * d[0] + (row[4] - col[4]) * d[1] + (row[5] - col[5]) * d[2]
            )
            inverse = lax.rsqrt(jnp.maximum(r2, 1e-30))
            r = r2 * inverse

            def slope(twice, per):
                t = per * r
                u = jnp.maximum(twice - t, 0.0)
                s = jnp.minimum(t, u)
                return s * (u + (u - s))

            h = row[8] + col[8]
            approach = (h * jnp.minimum(closing, 0.0)) * pl.reciprocal(r2 + h * h, approx=True)
            viscosity = (approach * (approach - (row[9] + col[9]))) * pl.reciprocal(
                row[10] + col[10], approx=True
            )
            weight = (row[11] + viscosity) * slope(row[6], row[7])
            weight = weight + (col[11] + viscosity) * slope(col[6], col[7])
            weight = weight * (inverse * col[12])
            for c in range(3):
                term = weight * d[c]
                acc[c] = term if acc[c] is None else acc[c] + term
        return acc

    def add(group, values):
        for c in range(3):
            total[group, c] = total[group, c] + values[c]

    number = work_items(count_v, items_v, items_s, ends, ends_v, ends_s, sem.at[1])
    run_items(number, BATCH_F, items_s, list_s, item, add)
    for c in range(3):
        sums[8 * c : 8 * c + 8, :] = row_sums(total, c, 3, reduced)


def spread_kernel(pushed, pushed_y, pushed_z, pushed_yz, coord, home, active, out):
    whole = joined(pushed, pushed_y, pushed_z, pushed_yz, coord, False)
    mine = picked(whole, home[0:1, :])
    slot = lax.broadcasted_iota(i32, (CELLS, 128), 1)
    for c in range(3):
        rows = lanes_to_cells(mine[8 * c : 8 * c + 8, :])
        rows = jnp.where(slot < active[...], rows, 0.0)
        out[c] = jnp.concatenate([rows, jnp.zeros((CELLS, 128), f32)], 1).reshape(BX, BY, BZ, 256)


VMEM_SPEC = pl.BlockSpec(memory_space=pltpu.VMEM)
SMEM_SPEC = pl.BlockSpec(memory_space=pltpu.SMEM)
PARAMS = pltpu.CompilerParams(vmem_limit_bytes=56 * 1024 * 1024)


def shape(*dims, dtype=f32):
    return jax.ShapeDtypeStruct(dims, dtype)


def call(kernel, inputs, outputs, in_specs=None, scratch=()):
    single = not isinstance(outputs, (list, tuple))
    return pl.pallas_call(
        kernel,
        out_shape=outputs,
        in_specs=in_specs or [VMEM_SPEC] * len(inputs),
        out_specs=VMEM_SPEC if single else [VMEM_SPEC] * len(outputs),
        scratch_shapes=list(scratch),
        compiler_params=PARAMS,
    )(*inputs)


def item_scratch():
    return [
        pltpu.VMEM((ITEM_ROWS, 128), i32), pltpu.SMEM((ITEM_ROWS, 128), i32),
        pltpu.VMEM((GROUPS, 128), f32), pltpu.VMEM((16, 128), f32), pltpu.SMEM((16, 128), f32),
    ]


def density_scratch():
    return [
        pltpu.VMEM((LIST_ROWS, 128), i32), pltpu.VMEM((16, 128), i32), pltpu.SMEM((LIST_ROWS, 128), i32),
        *item_scratch(), pltpu.VMEM((GROUPS * HELD, 128), f32), pltpu.VMEM((CELLS + 1, 4, 8, 128), f32),
        pltpu.VMEM((GROUPS, 1, 8, 128), f32), pltpu.VMEM((GROUPS, 128), f32),
        pltpu.VMEM((4, CELLS, 256), f32), pltpu.SemaphoreType.DMA((2,)),
    ]


def force_scratch():
    return [
        pltpu.SMEM((LIST_ROWS, 128), i32), *item_scratch(), pltpu.VMEM((GROUPS * HELD, 128), f32), pltpu.VMEM((CELLS + 1, 13, 8, 128), f32),
        pltpu.VMEM((GROUPS, 3, 8, 128), f32), pltpu.VMEM((GROUPS, 128), f32),
        pltpu.VMEM((10, CELLS, 256), f32), pltpu.SemaphoreType.DMA((2,)),
    ]


def ring(axis, by):
    devices = lax.axis_size(axis)
    return [(i, (i + by) % devices) for i in range(devices)]


def first_exchange(table, y_part, z_part, edge, low, high):
    y_in, z_in, edge_in = (
        lax.ppermute(part, ("gy", "gz"), pairs)
        for part, pairs in zip((y_part, z_part, edge), ACROSS)
    )
    low = jnp.concatenate([low, y_in[:, :8], z_in[:, :8], edge_in[:, :4]], 1)
    high = jnp.concatenate([high, y_in[:, 120:], z_in[:, 120:], edge_in[:, 60:]], 1)
    before = lax.ppermute(high, "gx", ring("gx", 1))
    after = lax.ppermute(low, "gx", ring("gx", -1))
    unused = jnp.zeros((ROWS, LANES - EXT), f32)
    return jnp.concatenate([table, y_in, z_in, edge_in, before, after, unused], 1)


ACROSS = (
    [(0, 2), (1, 3), (2, 0), (3, 1)],
    [(0, 1), (1, 0), (2, 3), (3, 2)],
    [(0, 3), (1, 2), (2, 1), (3, 0)],
)


def sent_across(sums):
    return [lax.ppermute(sums, ("gy", "gz"), pairs) for pairs in ACROSS]


def shared_sums(sums):
    plane = EY * EZ
    top = BX * plane
    before = lax.ppermute(sums[:, top : top + 2 * plane], "gx", ring("gx", 1))
    after = lax.ppermute(sums[:, : 2 * plane], "gx", ring("gx", -1))
    middle = sums[:, 2 * plane : top]
    return jnp.concatenate(
        [sums[:, : 2 * plane] + before, middle, sums[:, top:EXT] + after, sums[:, EXT:]], 1
    )


def returned_sums(sums):
    plane = EY * EZ
    top = BX * plane
    before = lax.ppermute(sums[:, top + plane : EXT], "gx", ring("gx", 1))
    after = lax.ppermute(sums[:, :plane], "gx", ring("gx", -1))
    return jnp.concatenate(
        [
            sums[:, :plane],
            sums[:, plane : 2 * plane] + before,
            sums[:, 2 * plane : top],
            sums[:, top : top + plane] + after,
            sums[:, top + plane :],
        ],
        1,
    )


def shards(pos, vel, mass, smooth, entropy, stored, particle_count, active_count, pair_side):
    coord_np, source_np = maps()
    coord, source = jnp.asarray(coord_np), jnp.asarray(source_np)
    home = jnp.asarray(home_lanes())
    count = particle_count.reshape(CELLS, 1)
    active = active_count.reshape(CELLS, 1)
    flags = jnp.concatenate(
        [
            pair_side.reshape(26, CELLS).astype(f32),
            active_count.reshape(1, CELLS).astype(f32),
            jnp.zeros((ROWS - FLAGS - 27, CELLS), f32),
        ],
        0,
    )
    inputs = (pos, vel, mass, smooth, entropy, stored, count, flags, jnp.asarray(sent_cells()))
    widths = (CELLS, 128, 128, 64, 16, 16)
    parts = first_exchange(*call(pack_kernel, inputs, [shape(ROWS, width) for width in widths]))
    inputs = (parts, coord, source, pos, mass, count)
    table, list_f, count_f, sums = call(
        density_kernel,
        inputs,
        [
            shape(ROWS, LANES), shape(LIST_ROWS, 128, dtype=i32), shape(16, 128, dtype=i32),
            shape(ACT, LANES),
        ],
        scratch=density_scratch(),
    )
    fresh = shared_sums(sums)
    inputs = (
        table, fresh, *sent_across(fresh), list_f, count_f, coord, home, pos, vel, mass, smooth, entropy, stored,
        count, active,
    )
    sums, density = call(
        force_kernel,
        inputs,
        [shape(24, LANES), shape(BX, BY, BZ, 256)],

        scratch=force_scratch(),
    )
    pushed = returned_sums(sums)
    inputs = (pushed, *sent_across(pushed), coord, home, active)
    acceleration = call(spread_kernel, inputs, shape(3, BX, BY, BZ, 256))
    return density, acceleration


def solution(mesh):
    cells = P("gx", "gy", "gz", None)
    vectors = P(None, "gx", "gy", "gz", None)
    counts = P("gx", "gy", "gz")
    in_specs = (
        vectors, vectors, cells, cells, cells, cells, counts, counts, P(None, "gx", "gy", "gz"),
    )
    return jax.shard_map(
        shards, mesh=mesh, in_specs=in_specs, out_specs=(cells, vectors), check_vma=False
    )
```

```python
import functools
import math

import jax
import jax.numpy as jnp
import numpy as np
from jax import lax
from jax.experimental import pallas as pl
from jax.experimental.pallas import tpu as pltpu
from jax.sharding import PartitionSpec as P

ACT = 8
BX, BY, BZ = 16, 4, 4
CELLS = BX * BY * BZ
EX, EY, EZ = BX + 2, BY + 2, BZ + 2
EXT = EX * EY * EZ
PLANE = EY * EZ
TOP = BX * PLANE
LANES = 768
TILES = LANES // 128
GROUPS = 2 * LANES
ROWS = 112
FLAGS = 80
LIVE = 106
SPAN = 3
WORDS = 9
ITEM_ROWS = 96
LIST_ROWS = 112
HELD = 13
BATCH_D = 8
BATCH_F = 8
NONE = CELLS
ADIABATIC = 5.0 / 3.0
HIGHEST = lax.Precision.HIGHEST
f32 = jnp.float32
i32 = jnp.int32

OFFSETS = [
    (a, b, c) for a in (-1, 0, 1) for b in (-1, 0, 1) for c in (-1, 0, 1) if (a, b, c) != (0, 0, 0)
]


def maps():
    coord = np.full((8, LANES), -9, np.int32)
    coord[:3] = -5
    source = np.full((8, LANES), -1, np.int32)
    for x in range(-1, BX + 1):
        for y in range(-1, BY + 1):
            for z in range(-1, BZ + 1):
                lane = ((x + 1) * EY + y + 1) * EZ + z + 1
                coord[0, lane], coord[1, lane], coord[2, lane] = x, y, z
                inside_y, inside_z = 0 <= y < BY, 0 <= z < BZ
                face_y = 0 if y == BY else 1
                face_z = 0 if z == BZ else 1
                def place(width_home, width_y, width_z, width_yz, starts, row):
                    if inside_y and inside_z:
                        return starts[0] + row * width_home + y * BZ + z
                    if inside_z:
                        return starts[1] + row * width_y + face_y * BZ + z
                    if inside_y:
                        return starts[2] + row * width_z + y * 2 + face_z
                    return starts[3] + row * width_yz + face_y * 2 + face_z

                if 0 <= x < BX:
                    at = place(16, 8, 8, 4, (0, 256, 384, 512), x)
                else:
                    base = 576 if x < 0 else 612
                    at = place(16, 8, 8, 4, (base, base + 16, base + 24, base + 32), 0)
                source[0, lane] = at
    return coord, source


def sent_cells():
    table = np.full((8, 384), -1, np.int32)
    for x in range(BX):
        for face in range(2):
            for z in range(BZ):
                table[0, x * 8 + face * BZ + z] = (x * BY + (0 if face == 0 else BY - 1)) * BZ + z
            for y in range(BY):
                table[0, 128 + x * 8 + y * 2 + face] = (x * BY + y) * BZ + (
                    0 if face == 0 else BZ - 1
                )
            for other in range(2):
                table[0, 256 + x * 4 + face * 2 + other] = (
                    x * BY + (0 if face == 0 else BY - 1)
                ) * BZ + (0 if other == 0 else BZ - 1)
    return table


def picked(values, source_row):
    count, size = values.shape
    rows = lax.broadcasted_iota(i32, (size, source_row.shape[1]), 0)
    chosen = (rows == source_row).astype(f32).astype(jnp.bfloat16)
    high = values.astype(jnp.bfloat16).astype(f32)
    rest = values - high
    middle = rest.astype(jnp.bfloat16).astype(f32)
    parts = jnp.concatenate([high, middle, rest - middle], 0).astype(jnp.bfloat16)
    out = jnp.dot(parts, chosen, preferred_element_type=f32)
    return out[:count] + out[count : 2 * count] + out[2 * count :]


def unit_rows():
    return (
        lax.broadcasted_iota(i32, (ACT, 128), 0) == lax.broadcasted_iota(i32, (ACT, 128), 1)
    ).astype(f32)


def cells_to_lanes(natural):
    return lax.dot_general(
        unit_rows(), natural[:, :128], (((1,), (1,)), ((), ())), precision=HIGHEST,
        preferred_element_type=f32,
    )


def lanes_to_cells(rows):
    return lax.dot_general(
        rows, unit_rows(), (((0,), (0,)), ((), ())), precision=HIGHEST, preferred_element_type=f32
    )


def live_mass(mass, count):
    slot = lax.broadcasted_iota(i32, (CELLS, 256), 1)
    return jnp.where(slot < count, mass, 0.0)


def pack_kernel(pos, vel, mass, smooth, entropy, stored, count, flags, sent, table, y_part, z_part, edge, low, high):
    fields = [pos[c].reshape(CELLS, 256) for c in range(3)]
    fields.append(live_mass(mass[...].reshape(CELLS, 256), count[...]))
    fields.append(smooth[...].reshape(CELLS, 256))
    fields += [vel[c].reshape(CELLS, 256) for c in range(3)]
    fields += [entropy[...].reshape(CELLS, 256), stored[...].reshape(CELLS, 256)]
    for f, field in enumerate(fields):
        table[8 * f : 8 * f + 8, :] = cells_to_lanes(field)
    table[FLAGS:ROWS, :] = flags[...]
    faces = picked(table[...], sent[0:1, :])
    y_part[...] = faces[:, :128]
    z_part[...] = faces[:, 128:256]
    edge[...] = faces[:, 256:320]
    low[...] = table[:, :16]
    high[...] = table[:, CELLS - 16 :]


def segment_units():
    row = lax.broadcasted_iota(i32, (24, 256), 0) % 8
    lane = lax.broadcasted_iota(i32, (24, 256), 1)
    return (row == lane // 128 * 4 + lane % 128 // 32).astype(f32)


def store_rows(target, feature, rows):
    high = rows.astype(jnp.bfloat16).astype(f32)
    rest = rows - high
    middle = rest.astype(jnp.bfloat16).astype(f32)
    parts = jnp.concatenate([high, middle, rest - middle], 0)
    spread = lax.dot_general(
        parts, segment_units(), (((0,), (0,)), ((), ())), preferred_element_type=f32
    )
    for group in range(2):
        for block in range(LANES // 8):
            at = (group * LANES + block * 8) * HELD + feature
            target[pl.ds(at, 8, stride=HELD), :] = spread[
                8 * block : 8 * block + 8, 128 * group : 128 * group + 128
            ]


def store_columns(target, feature, block, count, natural):
    part = lax.broadcasted_iota(i32, (8, 128), 1) // 32
    for half in range(2):
        slots = natural[:, 128 * half : 128 * half + 128]
        turns = [slots] + [pltpu.roll(slots, 32 * t, 1) for t in range(1, 4)]
        for k in range(4):
            value = turns[(0 - k) % 4]
            for r in range(1, 4):
                value = jnp.where(part == r, turns[(r - k) % 4], value)
            at = (block * 8 * count + feature) * 8 + half * 4 + k
            target.reshape((CELLS + 1) * count * 8, 128)[pl.ds(at, 8, stride=count * 8), :] = value


def build_lists(table, coord, list_d, list_f, count_d, count_f):
    row = lax.broadcasted_iota(i32, (8, LANES), 0)
    active = row.astype(f32) < table[LIVE : LIVE + 1, :]
    reach = 4.0 * table[32:40, :] * table[32:40, :] * 1.0001
    for_density = row % 4 == 3
    far = jnp.where(active, 0.0, 1e9)
    squares, inside, cells = [], [], []
    for c, (extent, step) in enumerate(((BX, BY * BZ), (BY, BZ), (BZ, 1))):
        p = table[8 * c : 8 * c + 8, :]
        squares.append({-1: p * p, 1: (1.0 - p) * (1.0 - p)})
        at = jnp.broadcast_to(coord[c : c + 1, :], (8, LANES))
        inside.append({o: (at + o >= 0) & (at + o < extent) for o in (-1, 0, 1)})
        cells.append(at * step)
    base = cells[0] + cells[1] + cells[2]

    def nearest(values):
        values = jnp.minimum(values, pltpu.roll(values, 1, 0))
        return jnp.minimum(values, pltpu.roll(values, 2, 0))

    entries = []
    kept = jnp.zeros((8, LANES), i32)
    center = 13
    offsets = OFFSETS[:center] + [(0, 0, 0)] + OFFSETS[center:]
    for k, (ox, oy, oz) in enumerate(offsets):
        away = far
        for c, o in enumerate((ox, oy, oz)):
            if o:
                away = away + squares[c][o]
        keep = inside[0][ox] & inside[1][oy] & inside[2][oz]
        if k != center:
            flag = FLAGS + (k if k < center else k - 1)
            keep = keep & (table[flag : flag + 1, :] > 0.5)
        over = jnp.where(
            for_density, nearest(away - reach), pltpu.roll(nearest(away - 1.0001), 7, 0)
        )
        keep = keep & (over <= 0.0)
        cell = base + ((ox * BY + oy) * BZ + oz + k * 1024)
        entries.append(jnp.where(keep, cell - kept * 1024, NONE))
        kept = kept + keep.astype(i32)
    for bit in range(5):
        step, mask = 1 << bit, 1024 << bit
        moves = [(e & mask) != 0 for e in entries]
        moved = []
        for p in range(27):
            e = jnp.where(moves[p], NONE, entries[p])
            if p + step < 27:
                e = jnp.where(moves[p + step], entries[p + step], e)
            moved.append(e)
        entries = moved
    entries = [e & 1023 for e in entries]
    for p in range(WORDS):
        word = entries[3 * p] + (entries[3 * p + 1] << 10) + (entries[3 * p + 2] << 20)
        for group in range(2):
            for t in range(TILES):
                at = (p * 2 + group) * TILES + t
                for first, target in ((3, list_d), (2, list_f)):
                    target[at : at + 1, :] = word[
                        first + 4 * group : first + 4 * group + 1, 128 * t : 128 * t + 128
                    ]
    for first, target, counted in ((3, list_d, count_d), (2, list_f, count_f)):
        target[WORDS * 2 * TILES :, :] = jnp.full((LIST_ROWS - WORDS * 2 * TILES, 128), NONE, i32)
        for group in range(2):
            for t in range(TILES):
                counted[group * TILES + t : group * TILES + t + 1, :] = kept[
                    first + 4 * group : first + 4 * group + 1, 128 * t : 128 * t + 128
                ]
        counted[2 * TILES :, :] = jnp.zeros((16 - 2 * TILES, 128), i32)


def work_items(counts, items_v, items_s, ends, ends_v, ends_s, sem):
    items = jnp.floor((counts[...] + SPAN - 1).astype(f32) * (1.00002 / SPAN))
    row = lax.broadcasted_iota(i32, (128, 128), 0)
    lane = lax.broadcasted_iota(i32, (128, 128), 1)
    within = jnp.dot(items, (row <= lane).astype(f32), preferred_element_type=f32)
    whole = jnp.broadcast_to(within[:, 127:128], (16, 128))
    earlier = (
        lax.broadcasted_iota(i32, (16, 16), 1) < lax.broadcasted_iota(i32, (16, 16), 0)
    ).astype(f32)
    end = within + jnp.dot(earlier, whole, precision=HIGHEST, preferred_element_type=f32)
    ends_v[...] = end
    copy = pltpu.make_async_copy(ends_v, ends_s, sem)
    copy.start()
    for t in range(2 * TILES):
        ends[128 * t : 128 * t + 128, :] = jnp.broadcast_to(end[t : t + 1, :], (128, 128)).T
    items_v[...] = jnp.full((ITEM_ROWS, 128), (GROUPS - 1) * 2049, i32)
    copy.wait()
    last = [ends_s[t, 127].astype(i32) for t in range(2 * TILES)]
    total = last[-1]
    lanes = lax.broadcasted_iota(i32, (8, 128), 1)

    def fill(j, _):
        first = j * 128
        index = first + lanes
        number = index.astype(f32)
        begin = jnp.int32(0)
        stop = jnp.int32(0)
        before = jnp.int32(0)
        for e in last:
            begin = begin + (e <= first).astype(i32)
            stop = stop + (e <= first + 127).astype(i32)
            before = jnp.where(e <= first, e, before)
        stop = jnp.minimum(stop + 1, 2 * TILES)

        def tile(t, carry):
            passed, start = carry
            for u in range(16):
                e = ends[pl.ds(pl.multiple_of(t * 128 + u * 8, 8), 8), :]
                over = e <= number
                passed = passed + jnp.where(over, 1.0, 0.0)
                start = jnp.maximum(start, jnp.where(over, e, 0.0))
            return passed, start

        zero = jnp.zeros((8, 128), f32)
        passed, start = lax.fori_loop(begin, stop, tile, (zero, zero))
        group = begin * 128 + jnp.sum(passed, 0, keepdims=True).astype(i32)
        start = jnp.maximum(jnp.max(start, 0, keepdims=True).astype(i32), before)
        code = group + ((index[0:1] - start) * GROUPS + group) * 2048
        items_v[pl.ds(j, 1), :] = jnp.where(index[0:1] < total, code, (GROUPS - 1) * 2049)
        return 0

    lax.fori_loop(0, (total + 127) >> 7, fill, 0)
    copy = pltpu.make_async_copy(items_v, items_s, sem)
    copy.start()
    copy.wait()
    return total


def run_items(total, batch, items, lists, item, add):
    per_row = 128 // batch
    bits = per_row.bit_length() - 1

    def take(turn):
        row, start = turn >> bits, (turn & (per_row - 1)) * batch
        codes = [items[row, start + u] for u in range(batch)]
        return codes, [lists[code >> 18, (code >> 11) & 127] for code in codes]

    def step(turn, carry):
        codes, words = carry
        results = []
        for code, word in zip(codes, words):
            group = code & 2047
            results.append((group, item(group, (word & 1023, (word >> 10) & 1023, word >> 20))))
        for group, values in results:
            add(group, values)
        return take(turn + 1)

    lax.fori_loop(0, (total + batch - 1) // batch, step, take(jnp.int32(0)))


def row_sums(tiles, part_index, count, reduced):
    def block(i, _):
        for u in range(16):
            value = None
            for s in range(8):
                at = ((i * 128 + u * 8) * count + part_index) * 8 + s
                part = tiles.reshape(GROUPS * count * 8, 128)[pl.ds(at, 8, stride=8 * count), :]
                value = part if value is None else value + part
            reduced[pl.ds(pl.multiple_of(i * 128 + u * 8, 8), 8), :] = value
        return 0

    lax.fori_loop(0, GROUPS // 128, block, 0)
    row = lax.broadcasted_iota(i32, (8, 128), 0)
    segment = lax.broadcasted_iota(i32, (8, 128), 1) // 32
    out = None
    for group in range(2):
        values = reduced[LANES * group : LANES * group + LANES, :]
        unit = (row == segment + 4 * group).astype(f32)
        high = values.astype(jnp.bfloat16).astype(f32)
        for part in (high, values - high):
            term = lax.dot_general(
                unit, part, (((1,), (1,)), ((), ())), preferred_element_type=f32
            )
            out = term if out is None else out + term
    return out


def density_kernel(
    parts, coord, source, pos, mass, count, table, list_f, count_f, sums, low, high,
    list_v, count_v, list_s, items_v, items_s, ends, ends_v, ends_s, rows, columns, total, reduced,
    natural, sem,
):
    table[...] = picked(parts[...], source[0:1, :])
    build_lists(table, coord, list_v, list_f, count_v, count_f)
    list_copy = pltpu.make_async_copy(list_v, list_s, sem.at[0])
    list_copy.start()
    place = coord[...].astype(f32)
    for c in range(3):
        store_rows(rows, c, table[8 * c : 8 * c + 8, :] + place[c : c + 1, :])
    smooth = table[32:40, :]
    home = lax.broadcasted_iota(i32, (8, LANES), 1) < EXT
    safe = jnp.where(home, smooth, 1.0)
    store_rows(rows, 3, 1.0 / safe)
    for c in range(3):
        natural[c] = pos[c].reshape(CELLS, 256)
    natural[3] = live_mass(mass[...].reshape(CELLS, 256), count[...])

    def fill_block(block):
        start = pl.ds(pl.multiple_of(block * 8, 8), 8)
        cell = block * 8 + lax.broadcasted_iota(i32, (8, 256), 0)
        for c, value in enumerate((cell // 16, (cell // 4) % 4, cell % 4)):
            store_columns(columns, c, block, 4, natural[c, start, :] + value.astype(f32))
        store_columns(columns, 3, block, 4, natural[3, start, :])

    def fill(step, _):
        for u in range(4):
            fill_block(step * 4 + u)
        return 0

    lax.fori_loop(0, CELLS // 32, fill, 0)
    columns[NONE] = jnp.zeros((4, 8, 128), f32)
    total[...] = jnp.zeros_like(total)
    list_copy.wait()

    def item(group, cells):
        row = [rows[pl.ds(group * HELD + f, 8, stride=0), :] for f in range(4)]
        acc = None
        for cell in cells:
            col = [columns[cell, f] for f in range(4)]
            d = [row[c] - col[c] for c in range(3)]
            r2 = d[0] * d[0] + d[1] * d[1] + d[2] * d[2]
            r = r2 * lax.rsqrt(jnp.maximum(r2, 1e-30))
            u = jnp.maximum(2.0 - r * row[3], 0.0)
            v = jnp.maximum(u - 1.0, 0.0)
            term = col[3] * (u * u * u - 4.0 * (v * v * v))
            acc = term if acc is None else acc + term
        return acc

    def add(group, value):
        total[group, 0] = total[group, 0] + value

    number = work_items(count_v, items_v, items_s, ends, ends_v, ends_s, sem.at[1])
    run_items(number, BATCH_D, items_s, list_s, item, add)
    scale = 1.0 / (4.0 * math.pi * safe * safe * safe)
    sums[...] = row_sums(total, 0, 1, reduced) * scale
    low[...] = sums[:, : 2 * PLANE]
    high[...] = sums[:, TOP:EXT]


def joined(sums, along_y, along_z, along_both, coord, shared):
    def matched(values, axis):
        step, extent = ((EZ, BY), (1, BZ))[axis - 1]
        position = coord[axis : axis + 1, :]
        low = position == 0
        high = position == extent - 1
        if shared:
            low = low | (position == -1)
            high = high | (position == extent)
        by = extent * step
        ahead = pltpu.roll(values, LANES - by, 1)
        behind = pltpu.roll(values, by, 1)
        return jnp.where(low, ahead, jnp.where(high, behind, 0.0))

    return (
        sums[...] + matched(along_y[...], 1) + matched(along_z[...], 2)
        + matched(matched(along_both[...], 1), 2)
    )


def home_lanes():
    cell = np.arange(CELLS)
    lane = ((cell // 16 + 1) * EY + (cell // 4) % 4 + 1) * EZ + cell % 4 + 1
    return np.tile(lane.astype(np.int32), (8, 1))


def state(entropy, density):
    pressure = entropy * jnp.exp(jnp.log(density) * (-1.0 / 3.0))
    return pressure, jnp.sqrt(ADIABATIC * pressure * density)


def force_kernel(
    table, fresh, fresh_y, fresh_z, fresh_yz, list_v, count_v, coord, home, pos, vel, mass, smooth, entropy, stored, count,
    active, sums, density, low, high, list_s, items_v, items_s, ends, ends_v, ends_s, rows, columns, total, reduced,
    natural, sem,
):
    list_copy = pltpu.make_async_copy(list_v, list_s, sem.at[0])
    list_copy.start()
    is_cell = lax.broadcasted_iota(i32, (8, LANES), 1) < EXT
    live = lax.broadcasted_iota(i32, (8, LANES), 0).astype(f32) < table[LIVE : LIVE + 1, :]
    place = coord[...].astype(f32)

    def field(f):
        return table[8 * f : 8 * f + 8, :]

    now = joined(fresh, fresh_y, fresh_z, fresh_yz, coord, True)
    rho = jnp.where(is_cell, jnp.where(live, now, field(9)), 1.0)
    row_h = jnp.where(is_cell, field(4), 1.0)
    row_p, row_s = state(field(8), rho)

    def features(h, sound, dens, pressure):
        a = math.sqrt(0.75 / math.pi) / (h * h)
        return 2.0 * a, a / h, 0.05 * h, 0.5 * sound, 2.0 * dens, pressure

    for c in range(3):
        store_rows(rows, c, field(c) + place[c : c + 1, :])
        store_rows(rows, 3 + c, 20.0 * field(5 + c))
    for f, value in enumerate(features(row_h, row_s, rho, row_p)):
        store_rows(rows, 6 + f, value)

    slot = lax.broadcasted_iota(i32, (CELLS, 128), 1)
    updated = lanes_to_cells(picked(rho, home[0:1, :]))
    old = stored[...].reshape(CELLS, 256)
    new = jnp.concatenate([jnp.where(slot < active[...], updated, old[:, :128]), old[:, 128:]], 1)
    density[...] = new.reshape(BX, BY, BZ, 256)
    for c in range(3):
        natural[c] = pos[c].reshape(CELLS, 256)
        natural[3 + c] = vel[c].reshape(CELLS, 256)
    natural[6] = live_mass(mass[...].reshape(CELLS, 256), count[...])
    natural[7] = smooth[...].reshape(CELLS, 256)
    natural[8] = entropy[...].reshape(CELLS, 256)
    natural[9] = new

    def fill_block(block):
        start = pl.ds(pl.multiple_of(block * 8, 8), 8)
        cell = block * 8 + lax.broadcasted_iota(i32, (8, 256), 0)
        for c, value in enumerate((cell // 16, (cell // 4) % 4, cell % 4)):
            store_columns(columns, c, block, 13, natural[c, start, :] + value.astype(f32))
            store_columns(columns, 3 + c, block, 13, 20.0 * natural[3 + c, start, :])
        dens = natural[9, start, :]
        pressure, sound = state(natural[8, start, :], dens)
        for f, value in enumerate(features(natural[7, start, :], sound, dens, pressure)):
            store_columns(columns, 6 + f, block, 13, value)
        store_columns(columns, 12, block, 13, natural[6, start, :])

    def fill(step, _):
        for u in range(2):
            fill_block(step * 2 + u)
        return 0

    lax.fori_loop(0, CELLS // 16, fill, 0)
    columns[NONE] = jnp.ones((13, 8, 128), f32)
    columns[NONE, 12] = jnp.zeros((8, 128), f32)
    total[...] = jnp.zeros_like(total)
    list_copy.wait()

    def item(group, cells):
        row = [rows[pl.ds(group * HELD + f, 8, stride=0), :] for f in range(12)]
        acc = [None] * 3
        for cell in cells:
            col = [columns[cell, f] for f in range(13)]
            d = [row[c] - col[c] for c in range(3)]
            r2 = d[0] * d[0] + d[1] * d[1] + d[2] * d[2]
            closing = (
                (row[3] - col[3]) * d[0] + (row[4] - col[4]) * d[1] + (row[5] - col[5]) * d[2]
            )
            inverse = lax.rsqrt(jnp.maximum(r2, 1e-30))
            r = r2 * inverse

            def slope(twice, per):
                t = per * r
                u = jnp.maximum(twice - t, 0.0)
                s = jnp.minimum(t, u)
                return s * (u + (u - s))

            h = row[8] + col[8]
            approach = (h * jnp.minimum(closing, 0.0)) * pl.reciprocal(r2 + h * h, approx=True)
            viscosity = (approach * (approach - (row[9] + col[9]))) * pl.reciprocal(
                row[10] + col[10], approx=True
            )
            weight = (row[11] + viscosity) * slope(row[6], row[7])
            weight = weight + (col[11] + viscosity) * slope(col[6], col[7])
            weight = weight * (inverse * col[12])
            for c in range(3):
                term = weight * d[c]
                acc[c] = term if acc[c] is None else acc[c] + term
        return acc

    def add(group, values):
        for c in range(3):
            total[group, c] = total[group, c] + values[c]

    number = work_items(count_v, items_v, items_s, ends, ends_v, ends_s, sem.at[1])
    run_items(number, BATCH_F, items_s, list_s, item, add)
    for c in range(3):
        sums[8 * c : 8 * c + 8, :] = row_sums(total, c, 3, reduced)
    low[...] = sums[:, :PLANE]
    high[...] = sums[:, TOP + PLANE : EXT]


def spread_kernel(pushed, pushed_y, pushed_z, pushed_yz, coord, home, active, out):
    whole = joined(pushed, pushed_y, pushed_z, pushed_yz, coord, False)
    mine = picked(whole, home[0:1, :])
    slot = lax.broadcasted_iota(i32, (CELLS, 128), 1)
    for c in range(3):
        rows = lanes_to_cells(mine[8 * c : 8 * c + 8, :])
        rows = jnp.where(slot < active[...], rows, 0.0)
        out[c] = jnp.concatenate([rows, jnp.zeros((CELLS, 128), f32)], 1).reshape(BX, BY, BZ, 256)


VMEM_SPEC = pl.BlockSpec(memory_space=pltpu.VMEM)
SMEM_SPEC = pl.BlockSpec(memory_space=pltpu.SMEM)
PARAMS = pltpu.CompilerParams(vmem_limit_bytes=56 * 1024 * 1024)


def shape(*dims, dtype=f32):
    return jax.ShapeDtypeStruct(dims, dtype)


def call(kernel, inputs, outputs, in_specs=None, scratch=()):
    single = not isinstance(outputs, (list, tuple))
    return pl.pallas_call(
        kernel,
        out_shape=outputs,
        in_specs=in_specs or [VMEM_SPEC] * len(inputs),
        out_specs=VMEM_SPEC if single else [VMEM_SPEC] * len(outputs),
        scratch_shapes=list(scratch),
        compiler_params=PARAMS,
    )(*inputs)


def item_scratch():
    return [
        pltpu.VMEM((ITEM_ROWS, 128), i32), pltpu.SMEM((ITEM_ROWS, 128), i32),
        pltpu.VMEM((GROUPS, 128), f32), pltpu.VMEM((16, 128), f32), pltpu.SMEM((16, 128), f32),
    ]


def density_scratch():
    return [
        pltpu.VMEM((LIST_ROWS, 128), i32), pltpu.VMEM((16, 128), i32), pltpu.SMEM((LIST_ROWS, 128), i32),
        *item_scratch(), pltpu.VMEM((GROUPS * HELD, 128), f32), pltpu.VMEM((CELLS + 1, 4, 8, 128), f32),
        pltpu.VMEM((GROUPS, 1, 8, 128), f32), pltpu.VMEM((GROUPS, 128), f32),
        pltpu.VMEM((4, CELLS, 256), f32), pltpu.SemaphoreType.DMA((2,)),
    ]


def force_scratch():
    return [
        pltpu.SMEM((LIST_ROWS, 128), i32), *item_scratch(), pltpu.VMEM((GROUPS * HELD, 128), f32), pltpu.VMEM((CELLS + 1, 13, 8, 128), f32),
        pltpu.VMEM((GROUPS, 3, 8, 128), f32), pltpu.VMEM((GROUPS, 128), f32),
        pltpu.VMEM((10, CELLS, 256), f32), pltpu.SemaphoreType.DMA((2,)),
    ]


def ring(axis, by):
    devices = lax.axis_size(axis)
    return [(i, (i + by) % devices) for i in range(devices)]


def first_exchange(table, y_part, z_part, edge, low, high):
    y_in, z_in, edge_in = (
        lax.ppermute(part, ("gy", "gz"), pairs)
        for part, pairs in zip((y_part, z_part, edge), ACROSS)
    )
    low = jnp.concatenate([low, y_in[:, :8], z_in[:, :8], edge_in[:, :4]], 1)
    high = jnp.concatenate([high, y_in[:, 120:], z_in[:, 120:], edge_in[:, 60:]], 1)
    before = lax.ppermute(high, "gx", ring("gx", 1))
    after = lax.ppermute(low, "gx", ring("gx", -1))
    unused = jnp.zeros((ROWS, LANES - EXT), f32)
    return jnp.concatenate([table, y_in, z_in, edge_in, before, after, unused], 1)


ACROSS = (
    [(0, 2), (1, 3), (2, 0), (3, 1)],
    [(0, 1), (1, 0), (2, 3), (3, 2)],
    [(0, 3), (1, 2), (2, 1), (3, 0)],
)


def sent_across(sums):
    return [lax.ppermute(sums, ("gy", "gz"), pairs) for pairs in ACROSS]


def shared_sums(sums, low, high):
    before = lax.ppermute(high, "gx", ring("gx", 1))
    after = lax.ppermute(low, "gx", ring("gx", -1))
    return jnp.concatenate([low + before, sums[:, 2 * PLANE : TOP], high + after, sums[:, EXT:]], 1)


def returned_sums(sums, low, high):
    before = lax.ppermute(high, "gx", ring("gx", 1))
    after = lax.ppermute(low, "gx", ring("gx", -1))
    return jnp.concatenate(
        [
            low,
            sums[:, PLANE : 2 * PLANE] + before,
            sums[:, 2 * PLANE : TOP],
            sums[:, TOP : TOP + PLANE] + after,
            sums[:, TOP + PLANE :],
        ],
        1,
    )


def shards(pos, vel, mass, smooth, entropy, stored, particle_count, active_count, pair_side):
    coord_np, source_np = maps()
    coord, source = jnp.asarray(coord_np), jnp.asarray(source_np)
    home = jnp.asarray(home_lanes())
    count = particle_count.reshape(CELLS, 1)
    active = active_count.reshape(CELLS, 1)
    flags = jnp.concatenate(
        [
            pair_side.reshape(26, CELLS).astype(f32),
            active_count.reshape(1, CELLS).astype(f32),
            jnp.zeros((ROWS - FLAGS - 27, CELLS), f32),
        ],
        0,
    )
    inputs = (pos, vel, mass, smooth, entropy, stored, count, flags, jnp.asarray(sent_cells()))
    widths = (CELLS, 128, 128, 64, 16, 16)
    parts = first_exchange(*call(pack_kernel, inputs, [shape(ROWS, width) for width in widths]))
    inputs = (parts, coord, source, pos, mass, count)
    table, list_f, count_f, sums, low, high = call(
        density_kernel,
        inputs,
        [
            shape(ROWS, LANES), shape(LIST_ROWS, 128, dtype=i32), shape(16, 128, dtype=i32),
            shape(ACT, LANES), shape(ACT, 2 * PLANE), shape(ACT, 2 * PLANE),
        ],
        scratch=density_scratch(),
    )
    fresh = shared_sums(sums, low, high)
    inputs = (
        table, fresh, *sent_across(fresh), list_f, count_f, coord, home, pos, vel, mass, smooth, entropy, stored,
        count, active,
    )
    sums, density, low, high = call(
        force_kernel,
        inputs,
        [shape(24, LANES), shape(BX, BY, BZ, 256), shape(24, PLANE), shape(24, PLANE)],

        scratch=force_scratch(),
    )
    pushed = returned_sums(sums, low, high)
    inputs = (pushed, *sent_across(pushed), coord, home, active)
    acceleration = call(spread_kernel, inputs, shape(3, BX, BY, BZ, 256))
    return density, acceleration


def solution(mesh):
    cells = P("gx", "gy", "gz", None)
    vectors = P(None, "gx", "gy", "gz", None)
    counts = P("gx", "gy", "gz")
    in_specs = (
        vectors, vectors, cells, cells, cells, cells, counts, counts, P(None, "gx", "gy", "gz"),
    )
    return jax.shard_map(
        shards, mesh=mesh, in_specs=in_specs, out_specs=(cells, vectors), check_vma=False
    )
```
